512 devices in a mesh: region: 2 (over x_lo), sector: 32 (over z, core), block: 8 (over x_hi, y).
Axes of the slice: x: 4 (x_hi: 2, x_lo: 2; x = x_hi * 2 + x_lo), y: 4, z: 16, core: 2. Of those that a mesh axis runs over, the one named last changes fastest.
Arguments:
- number_concentration: float32 [2, 64, 16, 256, 128], P('region', None, 'block', 'sector'), may hold values from 0.05 to 2
- frame_motion_vector: float32 [2, 3, 16, 256, 128], P('region', None, 'block', 'sector'), may hold values from -1 to 1
- strain_factor: float32 [2, 16, 256, 128], P('region', 'block', 'sector'), may hold values from 0.1 to 1
- splitting_kernel: float32 [64, 64], replicated, may hold values from -0.75 to 0.75
- merging_kernel: float32 [64, 64], replicated, may hold values from -0.75 to 0.75
- spinning_shift_history: int32 [2], replicated, may hold values from 0 to 255
- nearest_coverage_fraction: float32 [2], replicated, may hold values from 0.05 to 0.95
Outputs:
- evolved: float32 [2, 64, 16, 256, 128], P('region', None, 'block', 'sector')
The draws below stay inside these ranges and needn't reach their ends.
All inputs are finite; a program needn't handle non-finite values.
Results may differ from the reference program's by a relative error of at most 0.0001.
Values sent between devices are 32-bit elements; how exact they have to be, the bound alone decides.
No kernel may reach another device: no remote copies, remote signals or barrier semaphores. Data moves between devices by JAX's collectives and lax.ppermute only.
A program may use at most 64 MiB of HBM per device.

```python
import math
import jax
import jax.numpy as jnp
from jax import lax

DIAMETER_CLASSES = 64
AXL = 128
SUBSTEPS = 2
NAZ = 256
NR = 16


def shard_levels(key, shape, cuts, smallest, high):
    level = 1.0
    for position, shards_of in cuts:
        heights = jax.random.uniform(jax.random.fold_in(jax.random.fold_in(key, 6), position), (shards_of,), jnp.float32, smallest / len(cuts), high / len(cuts))
        level = level * jnp.repeat(jnp.exp(heights), shape[position] // shards_of).reshape((-1,) + (1,) * (len(shape) - 1 - position))
    return level


def centred(stream_key, dims, scale, bound, held_as=jnp.bfloat16):
    result = jax.random.normal(stream_key, dims, jnp.float32) * scale
    return jnp.minimum(jnp.maximum(result, -bound), bound).astype(held_as)


def setup_inputs(seed: int = 0) -> dict:
    arg_keys = jax.random.split(jax.random.key(seed), 8)
    number_concentration = jnp.clip(jnp.exp(math.log(2.0) - 3.6888794 * jax.random.uniform(arg_keys[0], (2, DIAMETER_CLASSES, NR, NAZ, AXL), jnp.float32) ** shard_levels(arg_keys[0], (2, DIAMETER_CLASSES, NR, NAZ, AXL), ((0, 2), (2, 8), (3, 32)), -0.2, 0.2)), 0.05, 2.0)
    frame_motion_vector = jnp.clip(jax.random.uniform(arg_keys[1], (2, 3, NR, NAZ, AXL), jnp.float32, -1.0, 1.0) * shard_levels(arg_keys[1], (2, 3, NR, NAZ, AXL), ((0, 2), (2, 8), (3, 32)), -0.4, 0.0), -1.0, 1.0)
    strain_factor = jnp.clip(jnp.exp(math.log(1.0) - 2.3025851 * jax.random.uniform(arg_keys[2], (2, NR, NAZ, AXL), jnp.float32) ** shard_levels(arg_keys[2], (2, NR, NAZ, AXL), ((0, 2), (1, 8), (2, 32)), -0.2, 0.2)), 0.1, 1.0)
    splitting_kernel = centred(arg_keys[3], (DIAMETER_CLASSES, DIAMETER_CLASSES), DIAMETER_CLASSES ** -0.5, 0.75, jnp.float32)
    merging_kernel = centred(arg_keys[4], (DIAMETER_CLASSES, DIAMETER_CLASSES), DIAMETER_CLASSES ** -0.5, 0.75, jnp.float32)
    spinning_shift_history = jax.random.randint(arg_keys[5], (SUBSTEPS,), 0, NAZ).astype(jnp.int32)
    nearest_coverage_fraction = jnp.clip(jax.random.uniform(arg_keys[6], (SUBSTEPS,), jnp.float32, 0.05, 0.95), 0.05, 0.95)
    return dict(number_concentration=number_concentration, frame_motion_vector=frame_motion_vector, strain_factor=strain_factor, splitting_kernel=splitting_kernel, merging_kernel=merging_kernel, spinning_shift_history=spinning_shift_history, nearest_coverage_fraction=nearest_coverage_fraction)


time_step = 0.2


def upstream_values(left, right, speed):
    return jnp.maximum(speed, 0.0) * left + jnp.minimum(speed, 0.0) * right


def reference(number_concentration, frame_motion_vector, strain_factor, splitting_kernel, merging_kernel, spinning_shift_history, nearest_coverage_fraction):
    azim_speed = 0.5 * (frame_motion_vector[:, 0] + jnp.roll(frame_motion_vector[:, 0], -1, axis=2))
    radial_inner = 0.5 * (frame_motion_vector[:, 1, :-1] + frame_motion_vector[:, 1, 1:])
    radial_speed = jnp.concatenate([radial_inner, frame_motion_vector[:, 1, -1:]], axis=1)
    axial_speed = 0.5 * (frame_motion_vector[:, 2] + jnp.roll(frame_motion_vector[:, 2], -1, axis=3))

    def transport(pair):
        cells, rim_values = pair
        outer = jnp.concatenate([cells[:, 1:], rim_values[:, None]], axis=1)
        rad_high = upstream_values(cells, outer, radial_speed)
        rad_low = jnp.concatenate([jnp.zeros_like(rad_high[:, :1]), rad_high[:, :-1]], axis=1)
        azim_high = upstream_values(cells, jnp.roll(cells, -1, axis=2), azim_speed)
        axial_high = upstream_values(cells, jnp.roll(cells, -1, axis=3), axial_speed)
        return (rad_high - rad_low) + (azim_high - jnp.roll(azim_high, 1, axis=2)) + (axial_high - jnp.roll(axial_high, 1, axis=3))

    field = number_concentration
    for substep in range(SUBSTEPS):
        shift_now = spinning_shift_history[substep]
        weight_now = nearest_coverage_fraction[substep]
        rotor_face = field[0, :, NR - 1]
        stator_face = field[1, :, NR - 1]
        stator_ghost = weight_now * jnp.roll(rotor_face, shift_now, axis=1) + (1.0 - weight_now) * jnp.roll(rotor_face, shift_now + 1, axis=1)
        rotor_ghost = weight_now * jnp.roll(stator_face, -shift_now, axis=1) + (1.0 - weight_now) * jnp.roll(stator_face, -shift_now - 1, axis=1)
        ghost = jnp.stack([rotor_ghost, stator_ghost])
        divergence = lax.map(transport, (jnp.moveaxis(field, 1, 0), jnp.moveaxis(ghost, 1, 0)))
        divergence = jnp.moveaxis(divergence, 0, 1)
        sources = []
        for region in range(2):
            unrolled_volumes = field[region].reshape(DIAMETER_CLASSES, -1)
            broken = jnp.dot(splitting_kernel, unrolled_volumes, precision=lax.Precision.HIGHEST, preferred_element_type=jnp.float32)
            joined_volumes = jnp.dot(merging_kernel, unrolled_volumes, precision=lax.Precision.HIGHEST, preferred_element_type=jnp.float32)
            term = strain_factor[region].reshape(-1) * broken + unrolled_volumes * joined_volumes
            sources.append(term.reshape(DIAMETER_CLASSES, NR, NAZ, AXL))
        field = field - time_step * divergence + time_step * jnp.stack(sources)
    return field
```

```python
import functools

import jax
import jax.numpy as jnp
from jax import lax
from jax.experimental import pallas as pl
from jax.experimental.pallas import tpu as pltpu
from jax.sharding import PartitionSpec as P

TIME_STEP = 0.2
AXES = ("region", "sector", "block")
SECTIONS = 64
CELLS = 8
ROWS = 2
AXIAL = 128
ROW_BYTES_ROWS = CELLS * SECTIONS
STRIDE = ROWS * CELLS


def device_number(region, sector, block):
    return (region * lax.axis_size("sector") + sector) * lax.axis_size("block") + block


def sector_pairs(step):
    count = lax.axis_size("sector")
    return [
        (device_number(r, s, b), device_number(r, (s + step) % count, b))
        for r in range(2)
        for s in range(count)
        for b in range(lax.axis_size("block"))
    ]


def block_pairs(step):
    count = lax.axis_size("block")
    return [
        (device_number(r, s, b), device_number(r, s, b + step))
        for r in range(2)
        for s in range(lax.axis_size("sector"))
        for b in range(count)
        if 0 <= b + step < count
    ]


def turn_pairs(sectors):
    count = lax.axis_size("sector")
    last = lax.axis_size("block") - 1
    return [
        (
            device_number(r, s, last),
            device_number(1 - r, (s + (sectors if r == 0 else -sectors)) % count, last),
        )
        for r in range(2)
        for s in range(count)
    ]


def line(index):
    return pl.ds(index * SECTIONS, SECTIONS)


def pack_kernel(field_ref, speed_ref, up_ref, down_ref, next_ref, prev_ref):
    for row, out_ref in ((0, down_ref), (1, up_ref)):
        for a in range(CELLS):
            cells = field_ref[pl.ds(row * CELLS + a, SECTIONS, stride=STRIDE), :]
            out_ref[line(a), :] = cells
            if a == 0:
                prev_ref[line(row), :] = cells
            if a == CELLS - 1:
                next_ref[line(row), :] = cells
        out_ref[pl.ds(ROW_BYTES_ROWS, CELLS), :] = speed_ref[pl.ds(STRIDE + row * CELLS, CELLS), :]
    tail = ROWS * SECTIONS
    for edge_ref, a in ((prev_ref, 0), (next_ref, CELLS - 1)):
        edge_ref[pl.ds(tail, 8), :] = jnp.zeros((8, AXIAL), jnp.float32)
        for row in range(ROWS):
            edge_ref[pl.ds(tail + row, 1), :] = speed_ref[pl.ds(row * CELLS + a, 1), :]


def pack(field, speeds):
    shape = lambda lines: jax.ShapeDtypeStruct((lines, AXIAL), jnp.float32)
    rim = ROW_BYTES_ROWS + CELLS
    edge = ROWS * SECTIONS + 8
    return pl.pallas_call(
        pack_kernel,
        out_shape=(shape(rim), shape(rim), shape(edge), shape(edge)),
        name="pack",
    )(field, speeds)


def split_halves(value):
    high = value.astype(jnp.bfloat16)
    low = (value - high.astype(jnp.float32)).astype(jnp.bfloat16)
    return high, low


def substep_kernel(
    substep,
    final,
    place_ref,
    shift_ref,
    weight_ref,
    up_ref,
    down_ref,
    prev_ref,
    next_ref,
    below_ref,
    above_ref,
    window_ref,
    below_speed_ref,
    above_speed_ref,
    prev_speed_ref,
    next_speed_ref,
    speed_ref,
    strain_ref,
    split_ref,
    merge_ref,
    *refs,
):
    if final:
        out_ref, coef_ref, top_ref = refs
    else:
        new_up_ref, new_down_ref, new_prev_ref, new_next_ref, coef_ref, top_ref = refs
    on_stator = place_ref[0] == 1
    first_block = place_ref[1] == 1
    last_block = place_ref[2] == 1
    weight = weight_ref[substep]

    @pl.when(last_block)
    def _():
        near = jnp.where(on_stator, weight, 1.0 - weight)
        within = shift_ref[substep] % CELLS
        odd = within % 2
        first = jnp.where(on_stator, 1 - odd + CELLS - (within - odd), odd)

        def window(index):
            position = first + index
            position = jnp.where(position >= CELLS + 2, position - (CELLS + 2), position)
            return window_ref[pl.ds(pl.multiple_of(position * SECTIONS, SECTIONS), SECTIONS), :]

        for a in range(CELLS):
            top_ref[line(a), :] = near * window(a + 1) + (1.0 - near) * window(a)

    @pl.when(jnp.logical_not(last_block))
    def _():
        top_ref[...] = above_ref[...]

    for row in range(ROWS):
        azim = speed_ref[pl.ds(row * CELLS, CELLS), :]
        azim_next = jnp.concatenate([azim[1:], next_speed_ref[pl.ds(row, 1), :]], axis=0)
        azim_prev = jnp.concatenate([prev_speed_ref[pl.ds(row, 1), :], azim[:-1]], axis=0)
        azim_high = 0.5 * (azim + azim_next)
        azim_low = 0.5 * (azim_prev + azim)
        radial = speed_ref[pl.ds(STRIDE + row * CELLS, CELLS), :]
        if row == 0:
            other = speed_ref[pl.ds(STRIDE + CELLS, CELLS), :]
            radial_high = 0.5 * (radial + other)
            radial_low = jnp.where(first_block, 0.0, 0.5 * (below_speed_ref[...] + radial))
        else:
            other = speed_ref[pl.ds(STRIDE, CELLS), :]
            radial_high = jnp.where(last_block, radial, 0.5 * (radial + above_speed_ref[...]))
            radial_low = 0.5 * (other + radial)
        axial = speed_ref[pl.ds(2 * STRIDE + row * CELLS, CELLS), :]
        axial_high = 0.5 * (axial + pltpu.roll(axial, AXIAL - 1, 1))
        axial_low = pltpu.roll(axial_high, 1, 1)
        own = 0.0
        place = row * CELLS
        for number, (high, low) in enumerate(
            ((radial_high, radial_low), (azim_high, azim_low), (axial_high, axial_low))
        ):
            own = own + jnp.maximum(high, 0.0) - jnp.minimum(low, 0.0)
            coef_ref[2 * number, pl.ds(place, CELLS), :] = -TIME_STEP * jnp.minimum(high, 0.0)
            coef_ref[2 * number + 1, pl.ds(place, CELLS), :] = TIME_STEP * jnp.maximum(low, 0.0)
        coef_ref[6, pl.ds(place, CELLS), :] = 1.0 - TIME_STEP * own
        coef_ref[7, pl.ds(place, CELLS), :] = TIME_STEP * strain_ref[pl.ds(place, CELLS), :]

    split_high, split_low = split_halves(split_ref[...])
    merge_high, merge_low = split_halves(TIME_STEP * merge_ref[...])
    both_high = jnp.concatenate([split_high, merge_high], axis=0)
    both_low = jnp.concatenate([split_low, merge_low], axis=0)
    left = jnp.concatenate([both_high, both_high, both_low], axis=1)

    for row in range(ROWS):
        own_ref = (down_ref, up_ref)[row]
        for pair in range(CELLS // 2):
            cells_of = [own_ref[line(2 * pair + i), :] for i in range(2)]
            wide = jnp.concatenate(cells_of, axis=1)
            high, low = split_halves(wide)
            right = jnp.concatenate([high, low, high], axis=0)
            products = jnp.dot(left, right, preferred_element_type=jnp.float32)
            for i in range(2):
                a = 2 * pair + i
                cells = cells_of[i]
                broken = products[:SECTIONS, i * AXIAL : (i + 1) * AXIAL]
                joined = products[SECTIONS:, i * AXIAL : (i + 1) * AXIAL]
                coef = lambda n: coef_ref[n, pl.ds(row * CELLS + a, 1), :]
                if row == 0:
                    outer, inner = up_ref[line(a), :], below_ref[line(a), :]
                else:
                    outer, inner = top_ref[line(a), :], down_ref[line(a), :]
                later = next_ref[line(row), :] if a == CELLS - 1 else own_ref[line(a + 1), :]
                earlier = prev_ref[line(row), :] if a == 0 else own_ref[line(a - 1), :]
                value = cells * (coef(6) + joined)
                value = value + coef(7) * broken
                value = value + (coef(0) * outer + coef(1) * inner)
                value = value + (coef(2) * later + coef(3) * earlier)
                value = value + (
                    coef(4) * pltpu.roll(cells, AXIAL - 1, 1) + coef(5) * pltpu.roll(cells, 1, 1)
                )
                if final:
                    out_ref[pl.ds(row * CELLS + a, SECTIONS, stride=STRIDE), :] = value
                else:
                    (new_down_ref, new_up_ref)[row][line(a), :] = value
                    if a == 0:
                        new_prev_ref[line(row), :] = value
                    if a == CELLS - 1:
                        new_next_ref[line(row), :] = value


def run_substep(substep, final, place, shifts, weights, *arrays):
    shape = lambda lines: jax.ShapeDtypeStruct((lines, AXIAL), jnp.float32)
    if final:
        out_shape = shape(SECTIONS * STRIDE)
    else:
        edge = ROWS * SECTIONS
        out_shape = (shape(ROW_BYTES_ROWS), shape(ROW_BYTES_ROWS), shape(edge), shape(edge))
    scalars = [pl.BlockSpec(memory_space=pltpu.SMEM)] * 3
    whole = [pl.BlockSpec(memory_space=pltpu.VMEM)] * len(arrays)
    return pl.pallas_call(
        functools.partial(substep_kernel, substep, final),
        out_shape=out_shape,
        in_specs=scalars + whole,
        scratch_shapes=[
            pltpu.VMEM((8, STRIDE, AXIAL), jnp.float32),
            pltpu.VMEM((ROW_BYTES_ROWS, AXIAL), jnp.float32),
        ],
        compiler_params=pltpu.CompilerParams(vmem_limit_bytes=32 * 1024 * 1024),
        name="substep",
    )(place, shifts, weights, *arrays)


def turned_window(row, shift):
    region = lax.axis_index("region")
    cells = row.reshape(CELLS, SECTIONS, AXIAL)

    def turn(sectors, within, cells):
        near, far = CELLS - within, within + 2
        near_start = jnp.where(region == 0, 0, within)
        far_start = jnp.where(region == 0, CELLS - far, 0)
        near_cells = lax.dynamic_slice_in_dim(cells, near_start, near, 0)
        far_cells = lax.dynamic_slice_in_dim(cells, far_start, far, 0)
        near_cells = lax.ppermute(near_cells, AXES, turn_pairs(sectors))
        far_cells = lax.ppermute(far_cells, AXES, turn_pairs(sectors + 1))
        return jnp.concatenate([near_cells, far_cells], 0)

    branches = [
        functools.partial(turn, sectors, within)
        for sectors in range(lax.axis_size("sector"))
        for within in range(0, CELLS, 2)
    ]
    return lax.switch(shift // 2, branches, cells).reshape((CELLS + 2) * SECTIONS, AXIAL)


def body(
    number_concentration,
    frame_motion_vector,
    strain_factor,
    splitting_kernel,
    merging_kernel,
    spinning_shift_history,
    nearest_coverage_fraction,
):
    field = number_concentration.reshape(SECTIONS * STRIDE, AXIAL)
    speeds = frame_motion_vector.reshape(3 * STRIDE, AXIAL)
    strain = strain_factor.reshape(STRIDE, AXIAL)
    block = lax.axis_index("block")
    place = jnp.stack(
        [
            lax.axis_index("region"),
            jnp.where(block == 0, 1, 0),
            jnp.where(block == lax.axis_size("block") - 1, 1, 0),
        ]
    ).astype(jnp.int32)
    up, down, to_next, to_prev = pack(field, speeds)
    from_prev = lax.ppermute(to_next, AXES, sector_pairs(1))
    from_next = lax.ppermute(to_prev, AXES, sector_pairs(-1))
    below = lax.ppermute(up, AXES, block_pairs(1))
    above = lax.ppermute(down, AXES, block_pairs(-1))
    window = turned_window(up[:ROW_BYTES_ROWS], spinning_shift_history[0])
    edge = ROWS * SECTIONS
    rim_speeds = (
        below[ROW_BYTES_ROWS:],
        above[ROW_BYTES_ROWS:],
        from_prev[edge:],
        from_next[edge:],
    )
    fixed = rim_speeds + (speeds, strain, splitting_kernel, merging_kernel)
    up, down, to_prev, to_next = run_substep(
        0,
        False,
        place,
        spinning_shift_history,
        nearest_coverage_fraction,
        up[:ROW_BYTES_ROWS],
        down[:ROW_BYTES_ROWS],
        from_prev[:edge],
        from_next[:edge],
        below[:ROW_BYTES_ROWS],
        above[:ROW_BYTES_ROWS],
        window,
        *fixed,
    )
    from_prev = lax.ppermute(to_next, AXES, sector_pairs(1))
    from_next = lax.ppermute(to_prev, AXES, sector_pairs(-1))
    below = lax.ppermute(up, AXES, block_pairs(1))
    above = lax.ppermute(down, AXES, block_pairs(-1))
    window = turned_window(up, spinning_shift_history[1])
    out = run_substep(
        1,
        True,
        place,
        spinning_shift_history,
        nearest_coverage_fraction,
        up,
        down,
        from_prev,
        from_next,
        below,
        above,
        window,
        *fixed,
    )
    return out.reshape(number_concentration.shape)


def solution(mesh):
    return jax.shard_map(
        body,
        mesh=mesh,
        in_specs=(
            P("region", None, "block", "sector", None),
            P("region", None, "block", "sector", None),
            P("region", "block", "sector", None),
            P(),
            P(),
            P(),
            P(),
        ),
        out_specs=P("region", None, "block", "sector", None),
        check_vma=False,
    )
```

```python
import functools

import jax
import jax.numpy as jnp
from jax import lax
from jax.experimental import pallas as pl
from jax.experimental.pallas import tpu as pltpu
from jax.sharding import PartitionSpec as P

TIME_STEP = 0.2
AXES = ("region", "sector", "block")
SECTIONS = 64
CELLS = 8
ROWS = 2
AXIAL = 128
ROW_BYTES_ROWS = CELLS * SECTIONS
STRIDE = ROWS * CELLS
HALF = SECTIONS // 2
SIDE = CELLS // 2


def device_number(region, sector, block):
    return (region * lax.axis_size("sector") + sector) * lax.axis_size("block") + block


def sector_pairs(step):
    count = lax.axis_size("sector")
    return [
        (device_number(r, s, b), device_number(r, (s + step) % count, b))
        for r in range(2)
        for s in range(count)
        for b in range(lax.axis_size("block"))
    ]


def block_pairs(step):
    count = lax.axis_size("block")
    return [
        (device_number(r, s, b), device_number(r, s, b + step))
        for r in range(2)
        for s in range(lax.axis_size("sector"))
        for b in range(count)
        if 0 <= b + step < count
    ]


def hop_pairs(relay):
    last = lax.axis_size("block") - 1
    return [
        (device_number(r, s, last), device_number(r, s, relay))
        for r in range(2)
        for s in range(lax.axis_size("sector"))
    ]


def turn_pairs(sectors, block):
    count = lax.axis_size("sector")
    last = lax.axis_size("block") - 1
    return [
        (
            device_number(r, s, block),
            device_number(1 - r, (s + (sectors if r == 0 else -sectors)) % count, last),
        )
        for r in range(2)
        for s in range(count)
    ]


def line(index):
    return pl.ds(index * SECTIONS, SECTIONS)


def turn_parts(place_ref, shift_ref, substep):
    on_stator = place_ref[0] == 1
    within = shift_ref[substep] % CELLS
    early = within < CELLS // 2
    upper = jnp.logical_xor(on_stator, early)
    return on_stator, within, early, upper


def store_turn(a, cells, upper, own_ref, far_ref, side_ref):
    own_ref[pl.ds(a * HALF, HALF), :] = cells[:HALF]
    far_ref[pl.ds(a * HALF, HALF), :] = cells[HALF:]
    wanted = upper if a >= SIDE else jnp.logical_not(upper)

    @pl.when(wanted)
    def _():
        side_ref[line(a % SIDE), :] = cells


def pack_kernel(
    place_ref, shift_ref, field_ref, speed_ref, up_ref, down_ref, next_ref, prev_ref, own_ref, far_ref, side_ref
):
    _, _, _, upper = turn_parts(place_ref, shift_ref, 0)
    for row, out_ref in ((0, down_ref), (1, up_ref)):
        for a in range(CELLS):
            cells = field_ref[pl.ds(row * CELLS + a, SECTIONS, stride=STRIDE), :]
            out_ref[line(a), :] = cells
            if a == 0:
                prev_ref[line(row), :] = cells
            if a == CELLS - 1:
                next_ref[line(row), :] = cells
            if row == ROWS - 1:
                store_turn(a, cells, upper, own_ref, far_ref, side_ref)
        out_ref[pl.ds(ROW_BYTES_ROWS, CELLS), :] = speed_ref[pl.ds(STRIDE + row * CELLS, CELLS), :]
    tail = ROWS * SECTIONS
    for edge_ref, a in ((prev_ref, 0), (next_ref, CELLS - 1)):
        edge_ref[pl.ds(tail, 8), :] = jnp.zeros((8, AXIAL), jnp.float32)
        for row in range(ROWS):
            edge_ref[pl.ds(tail + row, 1), :] = speed_ref[pl.ds(row * CELLS + a, 1), :]


def lines(count):
    return jax.ShapeDtypeStruct((count, AXIAL), jnp.float32)


TURN_SHAPES = (lines(CELLS * HALF), lines(CELLS * HALF), lines(SIDE * SECTIONS))


def pack(place, shifts, field, speeds):
    rim = lines(ROW_BYTES_ROWS + CELLS)
    edge = lines(ROWS * SECTIONS + 8)
    return pl.pallas_call(
        pack_kernel,
        out_shape=(rim, rim, edge, edge) + TURN_SHAPES,
        in_specs=[pl.BlockSpec(memory_space=pltpu.SMEM)] * 2 + [pl.BlockSpec(memory_space=pltpu.VMEM)] * 2,
        name="pack",
    )(place, shifts, field, speeds)


def split_halves(value):
    high = value.astype(jnp.bfloat16)
    low = (value - high.astype(jnp.float32)).astype(jnp.bfloat16)
    return high, low


def substep_kernel(
    substep,
    final,
    place_ref,
    shift_ref,
    weight_ref,
    up_ref,
    down_ref,
    prev_ref,
    next_ref,
    below_ref,
    above_ref,
    own_turn_ref,
    far_turn_ref,
    side_turn_ref,
    below_speed_ref,
    above_speed_ref,
    prev_speed_ref,
    next_speed_ref,
    speed_ref,
    strain_ref,
    split_ref,
    merge_ref,
    *refs,
):
    if final:
        out_ref, coef_ref, top_ref = refs
    else:
        new_up_ref, new_down_ref, new_prev_ref, new_next_ref = refs[:4]
        new_turn_refs = refs[4:7]
        coef_ref, top_ref = refs[7:]
        _, _, _, new_upper = turn_parts(place_ref, shift_ref, substep + 1)
    on_stator, within, early, _ = turn_parts(place_ref, shift_ref, substep)
    first_block = place_ref[1] == 1
    last_block = place_ref[2] == 1
    weight = weight_ref[substep]

    @pl.when(last_block)
    def _():
        near = jnp.where(on_stator, weight, 1.0 - weight)
        side_leads = on_stator == early
        first = jnp.where(on_stator, SIDE - 1 - within % SIDE, within % SIDE)

        def window(index):
            position = first + index
            from_side = jnp.where(side_leads, position < SIDE, position >= CELLS)
            row_cell = jnp.clip(position - jnp.where(side_leads, SIDE, 0), 0, CELLS - 1)
            side_cell = jnp.clip(position - jnp.where(side_leads, 0, CELLS), 0, SIDE - 1)
            row_at = pl.ds(pl.multiple_of(row_cell * HALF, HALF), HALF)
            row_cells = jnp.concatenate([own_turn_ref[row_at, :], far_turn_ref[row_at, :]], axis=0)
            side_at = pl.ds(pl.multiple_of(side_cell * SECTIONS, SECTIONS), SECTIONS)
            return jnp.where(from_side, side_turn_ref[side_at, :], row_cells)

        for a in range(CELLS):
            top_ref[line(a), :] = near * window(a + 1) + (1.0 - near) * window(a)

    @pl.when(jnp.logical_not(last_block))
    def _():
        top_ref[...] = above_ref[...]

    for row in range(ROWS):
        azim = speed_ref[pl.ds(row * CELLS, CELLS), :]
        azim_next = jnp.concatenate([azim[1:], next_speed_ref[pl.ds(row, 1), :]], axis=0)
        azim_prev = jnp.concatenate([prev_speed_ref[pl.ds(row, 1), :], azim[:-1]], axis=0)
        azim_high = 0.5 * (azim + azim_next)
        azim_low = 0.5 * (azim_prev + azim)
        radial = speed_ref[pl.ds(STRIDE + row * CELLS, CELLS), :]
        if row == 0:
            other = speed_ref[pl.ds(STRIDE + CELLS, CELLS), :]
            radial_high = 0.5 * (radial + other)
            radial_low = jnp.where(first_block, 0.0, 0.5 * (below_speed_ref[...] + radial))
        else:
            other = speed_ref[pl.ds(STRIDE, CELLS), :]
            radial_high = jnp.where(last_block, radial, 0.5 * (radial + above_speed_ref[...]))
            radial_low = 0.5 * (other + radial)
        axial = speed_ref[pl.ds(2 * STRIDE + row * CELLS, CELLS), :]
        axial_high = 0.5 * (axial + pltpu.roll(axial, AXIAL - 1, 1))
        axial_low = pltpu.roll(axial_high, 1, 1)
        own = 0.0
        place = row * CELLS
        for number, (high, low) in enumerate(
            ((radial_high, radial_low), (azim_high, azim_low), (axial_high, axial_low))
        ):
            own = own + jnp.maximum(high, 0.0) - jnp.minimum(low, 0.0)
            coef_ref[2 * number, pl.ds(place, CELLS), :] = -TIME_STEP * jnp.minimum(high, 0.0)
            coef_ref[2 * number + 1, pl.ds(place, CELLS), :] = TIME_STEP * jnp.maximum(low, 0.0)
        coef_ref[6, pl.ds(place, CELLS), :] = 1.0 - TIME_STEP * own
        coef_ref[7, pl.ds(place, CELLS), :] = TIME_STEP * strain_ref[pl.ds(place, CELLS), :]

    split_high, split_low = split_halves(split_ref[...])
    merge_high, merge_low = split_halves(TIME_STEP * merge_ref[...])
    both_high = jnp.concatenate([split_high, merge_high], axis=0)
    both_low = jnp.concatenate([split_low, merge_low], axis=0)
    left = jnp.concatenate([both_high, both_high, both_low], axis=1)

    for row in range(ROWS):
        own_ref = (down_ref, up_ref)[row]
        for pair in range(CELLS // 2):
            cells_of = [own_ref[line(2 * pair + i), :] for i in range(2)]
            wide = jnp.concatenate(cells_of, axis=1)
            high, low = split_halves(wide)
            right = jnp.concatenate([high, low, high], axis=0)
            products = jnp.dot(left, right, preferred_element_type=jnp.float32)
            for i in range(2):
                a = 2 * pair + i
                cells = cells_of[i]
                broken = products[:SECTIONS, i * AXIAL : (i + 1) * AXIAL]
                joined = products[SECTIONS:, i * AXIAL : (i + 1) * AXIAL]
                coef = lambda n: coef_ref[n, pl.ds(row * CELLS + a, 1), :]
                if row == 0:
                    outer, inner = up_ref[line(a), :], below_ref[line(a), :]
                else:
                    outer, inner = top_ref[line(a), :], down_ref[line(a), :]
                later = next_ref[line(row), :] if a == CELLS - 1 else own_ref[line(a + 1), :]
                earlier = prev_ref[line(row), :] if a == 0 else own_ref[line(a - 1), :]
                value = cells * (coef(6) + joined)
                value = value + coef(7) * broken
                value = value + (coef(0) * outer + coef(1) * inner)
                value = value + (coef(2) * later + coef(3) * earlier)
                value = value + (
                    coef(4) * pltpu.roll(cells, AXIAL - 1, 1) + coef(5) * pltpu.roll(cells, 1, 1)
                )
                if final:
                    out_ref[pl.ds(row * CELLS + a, SECTIONS, stride=STRIDE), :] = value
                else:
                    (new_down_ref, new_up_ref)[row][line(a), :] = value
                    if a == 0:
                        new_prev_ref[line(row), :] = value
                    if a == CELLS - 1:
                        new_next_ref[line(row), :] = value
                    if row == ROWS - 1:
                        store_turn(a, value, new_upper, *new_turn_refs)


def run_substep(substep, final, place, shifts, weights, *arrays):
    if final:
        out_shape = lines(SECTIONS * STRIDE)
    else:
        edge = ROWS * SECTIONS
        out_shape = (lines(ROW_BYTES_ROWS), lines(ROW_BYTES_ROWS), lines(edge), lines(edge)) + TURN_SHAPES
    scalars = [pl.BlockSpec(memory_space=pltpu.SMEM)] * 3
    whole = [pl.BlockSpec(memory_space=pltpu.VMEM)] * len(arrays)
    return pl.pallas_call(
        functools.partial(substep_kernel, substep, final),
        out_shape=out_shape,
        in_specs=scalars + whole,
        scratch_shapes=[
            pltpu.VMEM((8, STRIDE, AXIAL), jnp.float32),
            pltpu.VMEM((ROW_BYTES_ROWS, AXIAL), jnp.float32),
        ],
        compiler_params=pltpu.CompilerParams(vmem_limit_bytes=32 * 1024 * 1024),
        name="substep",
    )(place, shifts, weights, *arrays)


def relay_blocks():
    count = lax.axis_size("block")
    return count - 4, count - 2


def turned(shift, own, far, side, *before):
    far_relay, side_relay = relay_blocks()
    last = lax.axis_size("block") - 1
    far = lax.ppermute(far, AXES, hop_pairs(far_relay))
    side = lax.ppermute(side, AXES, hop_pairs(side_relay))
    (own, far, side), before = lax.optimization_barrier(((own, far, side), before))

    def turn(half_sectors, own, far, side):
        row_sectors = (half_sectors + 1) // 2
        side_sectors = half_sectors // 2 * 2 + 1 - row_sectors
        far = lax.ppermute(far, AXES, turn_pairs(row_sectors, far_relay))
        side = lax.ppermute(side, AXES, turn_pairs(side_sectors, side_relay))
        own = lax.ppermute(own, AXES, turn_pairs(row_sectors, last))
        return own, far, side

    def choose(low, count, *parts):
        if count == 1:
            return turn(low, *parts)
        middle = low + count // 2
        return lax.cond(
            shift < middle * SIDE,
            functools.partial(choose, low, middle - low),
            functools.partial(choose, middle, low + count - middle),
            *parts,
        )

    return choose(0, 2 * lax.axis_size("sector"), own, far, side), before


def body(
    number_concentration,
    frame_motion_vector,
    strain_factor,
    splitting_kernel,
    merging_kernel,
    spinning_shift_history,
    nearest_coverage_fraction,
):
    field = number_concentration.reshape(SECTIONS * STRIDE, AXIAL)
    speeds = frame_motion_vector.reshape(3 * STRIDE, AXIAL)
    strain = strain_factor.reshape(STRIDE, AXIAL)
    block = lax.axis_index("block")
    place = jnp.stack(
        [
            lax.axis_index("region"),
            jnp.where(block == 0, 1, 0),
            jnp.where(block == lax.axis_size("block") - 1, 1, 0),
        ]
    ).astype(jnp.int32)
    up, down, to_next, to_prev, *turning = pack(place, spinning_shift_history, field, speeds)
    from_prev = lax.ppermute(to_next, AXES, sector_pairs(1))
    from_next = lax.ppermute(to_prev, AXES, sector_pairs(-1))
    below = lax.ppermute(up, AXES, block_pairs(1))
    above = lax.ppermute(down, AXES, block_pairs(-1))
    across, (from_prev, from_next) = turned(spinning_shift_history[0], *turning, from_prev, from_next)
    edge = ROWS * SECTIONS
    rim_speeds = (
        below[ROW_BYTES_ROWS:],
        above[ROW_BYTES_ROWS:],
        from_prev[edge:],
        from_next[edge:],
    )
    fixed = rim_speeds + (speeds, strain, splitting_kernel, merging_kernel)
    up, down, to_prev, to_next, *turning = run_substep(
        0,
        False,
        place,
        spinning_shift_history,
        nearest_coverage_fraction,
        up[:ROW_BYTES_ROWS],
        down[:ROW_BYTES_ROWS],
        from_prev[:edge],
        from_next[:edge],
        below[:ROW_BYTES_ROWS],
        above[:ROW_BYTES_ROWS],
        *across,
        *fixed,
    )
    from_prev = lax.ppermute(to_next, AXES, sector_pairs(1))
    from_next = lax.ppermute(to_prev, AXES, sector_pairs(-1))
    below = lax.ppermute(up, AXES, block_pairs(1))
    above = lax.ppermute(down, AXES, block_pairs(-1))
    across, (from_prev, from_next) = turned(spinning_shift_history[1], *turning, from_prev, from_next)
    out = run_substep(
        1,
        True,
        place,
        spinning_shift_history,
        nearest_coverage_fraction,
        up,
        down,
        from_prev,
        from_next,
        below,
        above,
        *across,
        *fixed,
    )
    return out.reshape(number_concentration.shape)


def solution(mesh):
    return jax.shard_map(
        body,
        mesh=mesh,
        in_specs=(
            P("region", None, "block", "sector", None),
            P("region", None, "block", "sector", None),
            P("region", "block", "sector", None),
            P(),
            P(),
            P(),
            P(),
        ),
        out_specs=P("region", None, "block", "sector", None),
        check_vma=False,
    )
```

```python
import functools

import jax
import jax.numpy as jnp
from jax import lax
from jax.experimental import pallas as pl
from jax.experimental.pallas import tpu as pltpu
from jax.sharding import PartitionSpec as P

TIME_STEP = 0.2
AXES = ("region", "sector", "block")
SECTIONS = 64
CELLS = 8
ROWS = 2
AXIAL = 128
ROW_BYTES_ROWS = CELLS * SECTIONS
STRIDE = ROWS * CELLS
OWN = 40
CROSS = SECTIONS - OWN
DIRECT_CHIPS = 1
EDGE = ROW_BYTES_ROWS + SECTIONS


def device_number(region, sector, block):
    return (region * lax.axis_size("sector") + sector) * lax.axis_size("block") + block


def sector_pairs(step):
    count = lax.axis_size("sector")
    return [
        (device_number(r, s, b), device_number(r, (s + step) % count, b))
        for r in range(2)
        for s in range(count)
        for b in range(lax.axis_size("block"))
    ]


def block_pairs(step):
    count = lax.axis_size("block")
    return [
        (device_number(r, s, b), device_number(r, s, b + step))
        for r in range(2)
        for s in range(lax.axis_size("sector"))
        for b in range(count)
        if 0 <= b + step < count
    ]


def turn_pairs(sectors, across):
    count = lax.axis_size("sector")
    last = lax.axis_size("block") - 1
    return [
        (
            device_number(r, s, last),
            device_number(1 - r if across else r, (s + (sectors if (r == 0) == across else -sectors)) % count, last),
        )
        for r in range(2)
        for s in range(count)
    ]


def line(index):
    return pl.ds(index * SECTIONS, SECTIONS)


def pack_kernel(field_ref, speed_ref, up_ref, down_ref, next_ref, prev_ref):
    for row, out_ref in ((0, down_ref), (1, up_ref)):
        for a in range(CELLS):
            cells = field_ref[pl.ds(row * CELLS + a, SECTIONS, stride=STRIDE), :]
            store_cells(row, a, cells, up_ref, down_ref, next_ref, prev_ref)
        out_ref[pl.ds(ROW_BYTES_ROWS, CELLS), :] = speed_ref[pl.ds(STRIDE + row * CELLS, CELLS), :]
    for edge_ref, a in ((prev_ref, 0), (next_ref, CELLS - 1)):
        edge_ref[pl.ds(EDGE, 8), :] = jnp.zeros((8, AXIAL), jnp.float32)
        for row in range(ROWS):
            edge_ref[pl.ds(EDGE + row, 1), :] = speed_ref[pl.ds(row * CELLS + a, 1), :]


def store_cells(row, a, cells, up_ref, down_ref, next_ref, prev_ref):
    if row == ROWS - 1:
        for out_ref in (up_ref, next_ref, prev_ref):
            out_ref[line(a), :] = cells
    else:
        down_ref[line(a), :] = cells
        if a == 0:
            prev_ref[line(CELLS), :] = cells
        if a == CELLS - 1:
            next_ref[line(CELLS), :] = cells


def lines(count):
    return jax.ShapeDtypeStruct((count, AXIAL), jnp.float32)


def vmem(count):
    return [pl.BlockSpec(memory_space=pltpu.VMEM)] * count


def pack(field, speeds):
    rim = lines(ROW_BYTES_ROWS + CELLS)
    edge = lines(EDGE + 8)
    return pl.pallas_call(
        pack_kernel,
        out_shape=(rim, rim, edge, edge),
        in_specs=vmem(2),
        out_specs=tuple(vmem(4)),
        name="pack",
    )(field, speeds)


def align_kernel(substep, shift_ref, weight_ref, own_ref, prev_ref, next_ref, direct_ref, cross_ref, row_ref):
    @pl.when(lax.axis_index("block") == lax.axis_size("block") - 1)
    def _():
        on_stator = lax.axis_index("region") == 1
        residual = (shift_ref[substep] + CELLS) % STRIDE - CELLS
        weight = weight_ref[substep]
        for place, part_ref in enumerate((prev_ref, own_ref, next_ref)):
            row_ref[pl.ds(place * ROW_BYTES_ROWS, ROW_BYTES_ROWS), :] = part_ref[pl.ds(0, ROW_BYTES_ROWS), :]
        first = CELLS + jnp.where(on_stator, residual, -residual - 1)
        later_weight = jnp.where(on_stator, 1.0 - weight, weight)

        def cell(index):
            return row_ref[pl.ds(pl.multiple_of((first + index) * SECTIONS, SECTIONS), SECTIONS), :]

        for a in range(CELLS):
            ghost = later_weight * cell(a + 1) + (1.0 - later_weight) * cell(a)
            direct_ref[pl.ds(a * OWN, OWN), :] = ghost[:OWN]
            cross_ref[pl.ds(a * CROSS, CROSS), :] = ghost[OWN:]


def align(substep, shifts, weights, own, from_prev, from_next):
    return pl.pallas_call(
        functools.partial(align_kernel, substep),
        out_shape=(lines(CELLS * OWN), lines(CELLS * CROSS)),
        in_specs=[pl.BlockSpec(memory_space=pltpu.SMEM)] * 2 + vmem(3),
        out_specs=tuple(vmem(2)),
        scratch_shapes=[pltpu.VMEM((3 * ROW_BYTES_ROWS, AXIAL), jnp.float32)],
        name="align",
    )(shifts, weights, own, from_prev, from_next)


def split_halves(value):
    high = value.astype(jnp.bfloat16)
    low = (value - high.astype(jnp.float32)).astype(jnp.bfloat16)
    return high, low


def substep_kernel(
    final,
    up_ref,
    down_ref,
    prev_ref,
    next_ref,
    below_ref,
    above_ref,
    direct_ref,
    cross_ref,
    prev_rim_ref,
    next_rim_ref,
    below_rim_ref,
    above_rim_ref,
    speed_ref,
    strain_ref,
    split_ref,
    merge_ref,
    *refs,
):
    if final:
        out_ref, coef_ref, top_ref = refs
    else:
        *new_refs, coef_ref, top_ref = refs
    block = lax.axis_index("block")
    first_block = block == 0
    last_block = block == lax.axis_size("block") - 1
    below_speed = below_rim_ref[pl.ds(ROW_BYTES_ROWS, CELLS), :]
    above_speed = above_rim_ref[pl.ds(ROW_BYTES_ROWS, CELLS), :]

    @pl.when(last_block)
    def _():
        for a in range(CELLS):
            top_ref[pl.ds(a * SECTIONS, OWN), :] = direct_ref[pl.ds(a * OWN, OWN), :]
            top_ref[pl.ds(a * SECTIONS + OWN, CROSS), :] = cross_ref[pl.ds(a * CROSS, CROSS), :]

    @pl.when(jnp.logical_not(last_block))
    def _():
        top_ref[...] = above_ref[pl.ds(0, ROW_BYTES_ROWS), :]

    for row in range(ROWS):
        azim = speed_ref[pl.ds(row * CELLS, CELLS), :]
        azim_next = jnp.concatenate([azim[1:], next_rim_ref[pl.ds(EDGE + row, 1), :]], axis=0)
        azim_prev = jnp.concatenate([prev_rim_ref[pl.ds(EDGE + row, 1), :], azim[:-1]], axis=0)
        azim_high = 0.5 * (azim + azim_next)
        azim_low = 0.5 * (azim_prev + azim)
        radial = speed_ref[pl.ds(STRIDE + row * CELLS, CELLS), :]
        if row == 0:
            other = speed_ref[pl.ds(STRIDE + CELLS, CELLS), :]
            radial_high = 0.5 * (radial + other)
            radial_low = jnp.where(first_block, 0.0, 0.5 * (below_speed + radial))
        else:
            other = speed_ref[pl.ds(STRIDE, CELLS), :]
            radial_high = jnp.where(last_block, radial, 0.5 * (radial + above_speed))
            radial_low = 0.5 * (other + radial)
        axial = speed_ref[pl.ds(2 * STRIDE + row * CELLS, CELLS), :]
        axial_high = 0.5 * (axial + pltpu.roll(axial, AXIAL - 1, 1))
        axial_low = pltpu.roll(axial_high, 1, 1)
        own = 0.0
        place = row * CELLS
        for number, (high, low) in enumerate(
            ((radial_high, radial_low), (azim_high, azim_low), (axial_high, axial_low))
        ):
            own = own + jnp.maximum(high, 0.0) - jnp.minimum(low, 0.0)
            coef_ref[2 * number, pl.ds(place, CELLS), :] = -TIME_STEP * jnp.minimum(high, 0.0)
            coef_ref[2 * number + 1, pl.ds(place, CELLS), :] = TIME_STEP * jnp.maximum(low, 0.0)
        coef_ref[6, pl.ds(place, CELLS), :] = 1.0 - TIME_STEP * own
        coef_ref[7, pl.ds(place, CELLS), :] = TIME_STEP * strain_ref[pl.ds(place, CELLS), :]

    split_high, split_low = split_halves(split_ref[...])
    merge_high, merge_low = split_halves(TIME_STEP * merge_ref[...])
    both_high = jnp.concatenate([split_high, merge_high], axis=0)
    both_low = jnp.concatenate([split_low, merge_low], axis=0)
    left = jnp.concatenate([both_high, both_high, both_low], axis=1)

    for row in range(ROWS):
        own_ref = (down_ref, up_ref)[row]
        for pair in range(CELLS // 2):
            cells_of = [own_ref[line(2 * pair + i), :] for i in range(2)]
            wide = jnp.concatenate(cells_of, axis=1)
            high, low = split_halves(wide)
            right = jnp.concatenate([high, low, high], axis=0)
            products = jnp.dot(left, right, preferred_element_type=jnp.float32)
            for i in range(2):
                a = 2 * pair + i
                cells = cells_of[i]
                broken = products[:SECTIONS, i * AXIAL : (i + 1) * AXIAL]
                joined = products[SECTIONS:, i * AXIAL : (i + 1) * AXIAL]
                coef = lambda n: coef_ref[n, pl.ds(row * CELLS + a, 1), :]
                if row == 0:
                    outer, inner = up_ref[line(a), :], below_ref[line(a), :]
                else:
                    outer, inner = top_ref[line(a), :], down_ref[line(a), :]
                later = next_ref[line(0 if row else CELLS), :] if a == CELLS - 1 else own_ref[line(a + 1), :]
                earlier = prev_ref[line(CELLS - 1 if row else CELLS), :] if a == 0 else own_ref[line(a - 1), :]
                value = cells * (coef(6) + joined)
                value = value + coef(7) * broken
                value = value + (coef(0) * outer + coef(1) * inner)
                value = value + (coef(2) * later + coef(3) * earlier)
                value = value + (
                    coef(4) * pltpu.roll(cells, AXIAL - 1, 1) + coef(5) * pltpu.roll(cells, 1, 1)
                )
                if final:
                    out_ref[pl.ds(row * CELLS + a, SECTIONS, stride=STRIDE), :] = value
                else:
                    store_cells(row, a, value, *new_refs)


def run_substep(final, *arrays):
    if final:
        out_shape, out_specs = lines(SECTIONS * STRIDE), vmem(1)[0]
    else:
        out_shape = (lines(ROW_BYTES_ROWS), lines(ROW_BYTES_ROWS), lines(EDGE), lines(EDGE))
        out_specs = tuple(vmem(4))
    return pl.pallas_call(
        functools.partial(substep_kernel, final),
        out_shape=out_shape,
        in_specs=vmem(len(arrays)),
        out_specs=out_specs,
        scratch_shapes=[
            pltpu.VMEM((8, STRIDE, AXIAL), jnp.float32),
            pltpu.VMEM((ROW_BYTES_ROWS, AXIAL), jnp.float32),
        ],
        compiler_params=pltpu.CompilerParams(vmem_limit_bytes=32 * 1024 * 1024),
        name="substep",
    )(*arrays)


def turned(shift, direct, cross):
    count = lax.axis_size("sector") // 2

    def turn(chips, direct, cross):
        chips = chips % count
        distance = min(chips, count - chips)
        if distance <= DIRECT_CHIPS or 2 * distance == count:
            cross = lax.ppermute(cross, AXES, turn_pairs(2 * chips, True))
            direct = lax.ppermute(direct, AXES, turn_pairs(2 * chips, True))
        else:
            cross = lax.ppermute(cross, AXES, turn_pairs(0, True))
            direct = lax.ppermute(direct, AXES, turn_pairs(2 * chips, True))
            cross = lax.ppermute(cross, AXES, turn_pairs(2 * chips, False))
        return direct, cross

    def choose(low, high, direct, cross):
        if high - low == 1:
            return turn(low, direct, cross)
        middle = (low + high) // 2
        return lax.cond(
            shift < middle * STRIDE - CELLS,
            functools.partial(choose, low, middle),
            functools.partial(choose, middle, high),
            direct,
            cross,
        )

    return choose(0, count + 1, direct, cross)


def body(
    number_concentration,
    frame_motion_vector,
    strain_factor,
    splitting_kernel,
    merging_kernel,
    spinning_shift_history,
    nearest_coverage_fraction,
):
    field = number_concentration.reshape(SECTIONS * STRIDE, AXIAL)
    speeds = frame_motion_vector.reshape(3 * STRIDE, AXIAL)
    strain = strain_factor.reshape(STRIDE, AXIAL)
    shifts, weights = spinning_shift_history, nearest_coverage_fraction
    arrays = pack(field, speeds)
    rims = None
    for substep in range(2):
        up, down, to_next, to_prev = arrays
        from_prev = lax.ppermute(to_next, AXES, sector_pairs(1))
        from_next = lax.ppermute(to_prev, AXES, sector_pairs(-1))
        below = lax.ppermute(up, AXES, block_pairs(1))
        above = lax.ppermute(down, AXES, block_pairs(-1))
        direct, cross = align(substep, shifts, weights, up, from_prev, from_next)
        direct, cross = turned(shifts[substep], direct, cross)
        halos = (from_prev, from_next, below, above)
        rims = rims or halos
        arrays = run_substep(
            substep == 1,
            up,
            down,
            *halos,
            direct,
            cross,
            *rims,
            speeds,
            strain,
            splitting_kernel,
            merging_kernel,
        )
    return arrays.reshape(number_concentration.shape)


def solution(mesh):
    return jax.shard_map(
        body,
        mesh=mesh,
        in_specs=(
            P("region", None, "block", "sector", None),
            P("region", None, "block", "sector", None),
            P("region", "block", "sector", None),
            P(),
            P(),
            P(),
            P(),
        ),
        out_specs=P("region", None, "block", "sector", None),
        check_vma=False,
    )
```

```python
import functools

import jax
import jax.numpy as jnp
from jax import lax
from jax.experimental import pallas as pl
from jax.experimental.pallas import tpu as pltpu
from jax.sharding import PartitionSpec as P

TIME_STEP = 0.2
GRANT = 8 * 1024 * 1024
AXES = ("region", "sector", "block")
SECTIONS = 64
CELLS = 8
ROWS = 2
AXIAL = 128
ROW_BYTES_ROWS = CELLS * SECTIONS
STRIDE = ROWS * CELLS
OWN = 40
CROSS = SECTIONS - OWN
DIRECT_CHIPS = 1
EDGE = ROW_BYTES_ROWS + SECTIONS


def device_number(region, sector, block):
    return (region * lax.axis_size("sector") + sector) * lax.axis_size("block") + block


def swap_pairs(axis, first):
    sectors, blocks = lax.axis_size("sector"), lax.axis_size("block")
    pairs = []
    for r in range(2):
        for s in range(sectors):
            for b in range(blocks):
                if axis == "sector":
                    step = 1 if s % 2 == first else -1
                    to = device_number(r, (s + step) % sectors, b)
                else:
                    step = 1 if b % 2 == first else -1
                    if not 0 <= b + step < blocks:
                        continue
                    to = device_number(r, s, b + step)
                pairs.append((device_number(r, s, b), to))
    return pairs


def turn_pairs(sectors, across):
    count = lax.axis_size("sector")
    last = lax.axis_size("block") - 1
    return [
        (
            device_number(r, s, last),
            device_number(1 - r if across else r, (s + (sectors if (r == 0) == across else -sectors)) % count, last),
        )
        for r in range(2)
        for s in range(count)
    ]


def line(index):
    return pl.ds(index * SECTIONS, SECTIONS)


def is_even(axis):
    return lax.axis_index(axis) % 2 == 0


def pack_kernel(field_ref, speed_ref, *out_refs):
    for row in range(ROWS):
        cells = [field_ref[pl.ds(row * CELLS + a, SECTIONS, stride=STRIDE), :] for a in range(CELLS)]
        for a in range(CELLS):
            store_cells(row, a, cells[a], *out_refs)
    _, _, first_block_ref, second_block_ref, first_sector_ref, second_sector_ref = out_refs
    store_edge(lambda a: field_ref[pl.ds(a, SECTIONS, stride=STRIDE), :], first_sector_ref, second_sector_ref)
    even_block, even_sector = is_even("block"), is_even("sector")
    low, high = [speed_ref[pl.ds(STRIDE + row * CELLS, CELLS), :] for row in range(ROWS)]
    first_block_ref[pl.ds(ROW_BYTES_ROWS, CELLS), :] = jnp.where(even_block, high, low)
    second_block_ref[pl.ds(ROW_BYTES_ROWS, CELLS), :] = jnp.where(even_block, low, high)
    for edge_ref, last_cell in ((first_sector_ref, even_sector), (second_sector_ref, jnp.logical_not(even_sector))):
        edge_ref[pl.ds(EDGE, 8), :] = jnp.zeros((8, AXIAL), jnp.float32)
        for row in range(ROWS):
            a, z = [speed_ref[pl.ds(row * CELLS + place, 1), :] for place in (0, CELLS - 1)]
            edge_ref[pl.ds(EDGE + row, 1), :] = jnp.where(last_cell, z, a)


def store_cells(row, a, cells, low_ref, high_ref, first_block_ref, second_block_ref, first_sector_ref, second_sector_ref):
    (low_ref, high_ref)[row][line(a), :] = cells
    up_is_first = is_even("block")
    goes_first = up_is_first if row else jnp.logical_not(up_is_first)

    @pl.when(goes_first)
    def _():
        first_block_ref[line(a), :] = cells

    @pl.when(jnp.logical_not(goes_first))
    def _():
        second_block_ref[line(a), :] = cells

    if row == ROWS - 1:
        first_sector_ref[line(a), :] = cells
        second_sector_ref[line(a), :] = cells


def store_edge(cells, first_sector_ref, second_sector_ref):
    even = is_even("sector")
    a, z = cells(0), cells(CELLS - 1)
    first_sector_ref[line(CELLS), :] = jnp.where(even, z, a)
    second_sector_ref[line(CELLS), :] = jnp.where(even, a, z)


def lines(count):
    return jax.ShapeDtypeStruct((count, AXIAL), jnp.float32)


def vmem(count):
    return [pl.BlockSpec(memory_space=pltpu.VMEM)] * count


def pack(field, speeds):
    row = lines(ROW_BYTES_ROWS)
    rim = lines(ROW_BYTES_ROWS + CELLS)
    edge = lines(EDGE + 8)
    return pl.pallas_call(
        pack_kernel,
        out_shape=(row, row, rim, rim, edge, edge),
        in_specs=vmem(2),
        out_specs=tuple(vmem(6)),
        compiler_params=pltpu.CompilerParams(vmem_limit_bytes=GRANT),
        name="pack",
    )(field, speeds)


def align_kernel(substep, shift_ref, weight_ref, own_ref, first_ref, second_ref, direct_ref, cross_ref, row_ref):
    @pl.when(lax.axis_index("block") == lax.axis_size("block") - 1)
    def _():
        on_stator = lax.axis_index("region") == 1
        residual = (shift_ref[substep] + CELLS) % STRIDE - CELLS
        weight = weight_ref[substep]
        first_place = jnp.where(is_even("sector"), 2, 0)
        for place, part_ref in ((first_place, first_ref), (1, own_ref), (2 - first_place, second_ref)):
            start = pl.multiple_of(place * ROW_BYTES_ROWS, ROW_BYTES_ROWS)
            row_ref[pl.ds(start, ROW_BYTES_ROWS), :] = part_ref[pl.ds(0, ROW_BYTES_ROWS), :]
        first = CELLS + jnp.where(on_stator, residual, -residual - 1)
        later_weight = jnp.where(on_stator, 1.0 - weight, weight)

        def cell(index):
            return row_ref[pl.ds(pl.multiple_of((first + index) * SECTIONS, SECTIONS), SECTIONS), :]

        for a in range(CELLS):
            ghost = later_weight * cell(a + 1) + (1.0 - later_weight) * cell(a)
            direct_ref[pl.ds(a * OWN, OWN), :] = ghost[:OWN]
            cross_ref[pl.ds(a * CROSS, CROSS), :] = ghost[OWN:]


def align(substep, shifts, weights, own, first, second):
    return pl.pallas_call(
        functools.partial(align_kernel, substep),
        out_shape=(lines(CELLS * OWN), lines(CELLS * CROSS)),
        in_specs=[pl.BlockSpec(memory_space=pltpu.SMEM)] * 2 + vmem(3),
        out_specs=tuple(vmem(2)),
        scratch_shapes=[pltpu.VMEM((3 * ROW_BYTES_ROWS, AXIAL), jnp.float32)],
        compiler_params=pltpu.CompilerParams(vmem_limit_bytes=GRANT),
        name="align",
    )(shifts, weights, own, first, second)


def split_halves(value):
    high = value.astype(jnp.bfloat16)
    low = (value - high.astype(jnp.float32)).astype(jnp.bfloat16)
    return high, low


def substep_kernel(
    final,
    low_ref,
    high_ref,
    first_sector_ref,
    second_sector_ref,
    first_block_ref,
    second_block_ref,
    direct_ref,
    cross_ref,
    first_sector_rim_ref,
    second_sector_rim_ref,
    first_block_rim_ref,
    second_block_rim_ref,
    speed_ref,
    strain_ref,
    split_ref,
    merge_ref,
    *refs,
):
    if final:
        out_ref, coef_ref, top_ref = refs
    else:
        *new_refs, coef_ref, top_ref = refs
    block = lax.axis_index("block")
    first_block = block == 0
    last_block = block == lax.axis_size("block") - 1
    even_block, even_sector = is_even("block"), is_even("sector")

    def by_block(lines_of, first_ref=first_block_ref, second_ref=second_block_ref):
        one, two = first_ref[lines_of, :], second_ref[lines_of, :]
        return jnp.where(even_block, one, two), jnp.where(even_block, two, one)

    def by_sector(lines_of, first_ref=first_sector_ref, second_ref=second_sector_ref):
        one, two = first_ref[lines_of, :], second_ref[lines_of, :]
        return jnp.where(even_sector, one, two), jnp.where(even_sector, two, one)

    above_speed, below_speed = by_block(pl.ds(ROW_BYTES_ROWS, CELLS), first_block_rim_ref, second_block_rim_ref)

    @pl.when(last_block)
    def _():
        for a in range(CELLS):
            top_ref[pl.ds(a * SECTIONS, OWN), :] = direct_ref[pl.ds(a * OWN, OWN), :]
            top_ref[pl.ds(a * SECTIONS + OWN, CROSS), :] = cross_ref[pl.ds(a * CROSS, CROSS), :]

    @pl.when(jnp.logical_not(last_block))
    def _():
        for a in range(CELLS):
            top_ref[line(a), :] = by_block(line(a))[0]

    for row in range(ROWS):
        azim = speed_ref[pl.ds(row * CELLS, CELLS), :]
        after, before = by_sector(pl.ds(EDGE + row, 1), first_sector_rim_ref, second_sector_rim_ref)
        azim_next = jnp.concatenate([azim[1:], after], axis=0)
        azim_prev = jnp.concatenate([before, azim[:-1]], axis=0)
        azim_high = 0.5 * (azim + azim_next)
        azim_low = 0.5 * (azim_prev + azim)
        radial = speed_ref[pl.ds(STRIDE + row * CELLS, CELLS), :]
        if row == 0:
            other = speed_ref[pl.ds(STRIDE + CELLS, CELLS), :]
            radial_high = 0.5 * (radial + other)
            radial_low = jnp.where(first_block, 0.0, 0.5 * (below_speed + radial))
        else:
            other = speed_ref[pl.ds(STRIDE, CELLS), :]
            radial_high = jnp.where(last_block, radial, 0.5 * (radial + above_speed))
            radial_low = 0.5 * (other + radial)
        axial = speed_ref[pl.ds(2 * STRIDE + row * CELLS, CELLS), :]
        axial_high = 0.5 * (axial + pltpu.roll(axial, AXIAL - 1, 1))
        axial_low = pltpu.roll(axial_high, 1, 1)
        own = 0.0
        place = row * CELLS
        for number, (high, low) in enumerate(
            ((radial_high, radial_low), (azim_high, azim_low), (axial_high, axial_low))
        ):
            own = own + jnp.maximum(high, 0.0) - jnp.minimum(low, 0.0)
            coef_ref[2 * number, pl.ds(place, CELLS), :] = -TIME_STEP * jnp.minimum(high, 0.0)
            coef_ref[2 * number + 1, pl.ds(place, CELLS), :] = TIME_STEP * jnp.maximum(low, 0.0)
        coef_ref[6, pl.ds(place, CELLS), :] = 1.0 - TIME_STEP * own
        coef_ref[7, pl.ds(place, CELLS), :] = TIME_STEP * strain_ref[pl.ds(place, CELLS), :]

    split_high, split_low = split_halves(split_ref[...])
    merge_high, merge_low = split_halves(TIME_STEP * merge_ref[...])
    both_high = jnp.concatenate([split_high, merge_high], axis=0)
    both_low = jnp.concatenate([split_low, merge_low], axis=0)
    left = jnp.concatenate([both_high, both_high, both_low], axis=1)

    for row in range(ROWS):
        own_ref = (low_ref, high_ref)[row]
        for pair in range(CELLS // 2):
            cells_of = [own_ref[line(2 * pair + i), :] for i in range(2)]
            wide = jnp.concatenate(cells_of, axis=1)
            high, low = split_halves(wide)
            right = jnp.concatenate([high, low, high], axis=0)
            products = jnp.dot(left, right, preferred_element_type=jnp.float32)
            for i in range(2):
                a = 2 * pair + i
                cells = cells_of[i]
                broken = products[:SECTIONS, i * AXIAL : (i + 1) * AXIAL]
                joined = products[SECTIONS:, i * AXIAL : (i + 1) * AXIAL]
                coef = lambda n: coef_ref[n, pl.ds(row * CELLS + a, 1), :]
                if row == 0:
                    outer, inner = high_ref[line(a), :], by_block(line(a))[1]
                else:
                    outer, inner = top_ref[line(a), :], low_ref[line(a), :]
                if a == CELLS - 1:
                    later = by_sector(line(0 if row else CELLS))[0]
                else:
                    later = own_ref[line(a + 1), :]
                if a == 0:
                    earlier = by_sector(line(CELLS - 1 if row else CELLS))[1]
                else:
                    earlier = own_ref[line(a - 1), :]
                value = cells * (coef(6) + joined)
                value = value + coef(7) * broken
                value = value + (coef(0) * outer + coef(1) * inner)
                value = value + (coef(2) * later + coef(3) * earlier)
                value = value + (
                    coef(4) * pltpu.roll(cells, AXIAL - 1, 1) + coef(5) * pltpu.roll(cells, 1, 1)
                )
                if final:
                    out_ref[pl.ds(row * CELLS + a, SECTIONS, stride=STRIDE), :] = value
                else:
                    store_cells(row, a, value, *new_refs)
        if row == 0 and not final:
            store_edge(lambda a: new_refs[0][line(a), :], *new_refs[4:])


def run_substep(final, *arrays):
    if final:
        out_shape, out_specs = lines(SECTIONS * STRIDE), vmem(1)[0]
    else:
        out_shape = (lines(ROW_BYTES_ROWS),) * 4 + (lines(EDGE),) * 2
        out_specs = tuple(vmem(6))
    return pl.pallas_call(
        functools.partial(substep_kernel, final),
        out_shape=out_shape,
        in_specs=vmem(len(arrays)),
        out_specs=out_specs,
        scratch_shapes=[
            pltpu.VMEM((8, STRIDE, AXIAL), jnp.float32),
            pltpu.VMEM((ROW_BYTES_ROWS, AXIAL), jnp.float32),
        ],
        compiler_params=pltpu.CompilerParams(vmem_limit_bytes=GRANT),
        name="substep",
    )(*arrays)


def turned(shift, direct, cross):
    count = lax.axis_size("sector") // 2

    def turn(chips, direct, cross):
        chips = chips % count
        distance = min(chips, count - chips)
        if distance <= DIRECT_CHIPS or 2 * distance == count:
            cross = lax.ppermute(cross, AXES, turn_pairs(2 * chips, True))
            direct = lax.ppermute(direct, AXES, turn_pairs(2 * chips, True))
        else:
            cross = lax.ppermute(cross, AXES, turn_pairs(0, True))
            direct = lax.ppermute(direct, AXES, turn_pairs(2 * chips, True))
            cross = lax.ppermute(cross, AXES, turn_pairs(2 * chips, False))
        return direct, cross

    def choose(low, high, direct, cross):
        if high - low == 1:
            return turn(low, direct, cross)
        middle = (low + high) // 2
        return lax.cond(
            shift < middle * STRIDE - CELLS,
            functools.partial(choose, low, middle),
            functools.partial(choose, middle, high),
            direct,
            cross,
        )

    return choose(0, count + 1, direct, cross)


def body(
    number_concentration,
    frame_motion_vector,
    strain_factor,
    splitting_kernel,
    merging_kernel,
    spinning_shift_history,
    nearest_coverage_fraction,
):
    field = number_concentration.reshape(SECTIONS * STRIDE, AXIAL)
    speeds = frame_motion_vector.reshape(3 * STRIDE, AXIAL)
    strain = strain_factor.reshape(STRIDE, AXIAL)
    shifts, weights = spinning_shift_history, nearest_coverage_fraction
    arrays = pack(field, speeds)
    rims = None
    for substep in range(2):
        low, high, *sends = arrays
        swaps = [("block", 0), ("block", 1), ("sector", 0), ("sector", 1)]
        blocks_sectors = [lax.ppermute(sent, AXES, swap_pairs(*swap)) for sent, swap in zip(sends, swaps)]
        halos = blocks_sectors[2:] + blocks_sectors[:2]
        direct, cross = align(substep, shifts, weights, high, *halos[:2])
        direct, cross = turned(shifts[substep], direct, cross)
        rims = rims or halos
        arrays = run_substep(
            substep == 1,
            low,
            high,
            *halos,
            direct,
            cross,
            *rims,
            speeds,
            strain,
            splitting_kernel,
            merging_kernel,
        )
    return arrays.reshape(number_concentration.shape)


def solution(mesh):
    return jax.shard_map(
        body,
        mesh=mesh,
        in_specs=(
            P("region", None, "block", "sector", None),
            P("region", None, "block", "sector", None),
            P("region", "block", "sector", None),
            P(),
            P(),
            P(),
            P(),
        ),
        out_specs=P("region", None, "block", "sector", None),
        check_vma=False,
    )
```

```python
import functools

import jax
import jax.numpy as jnp
from jax import lax
from jax.experimental import pallas as pl
from jax.experimental.pallas import tpu as pltpu
from jax.sharding import PartitionSpec as P

TIME_STEP = 0.2
GRANT = 8 * 1024 * 1024
AXES = ("region", "sector", "block")
SECTIONS = 64
CELLS = 8
ROWS = 2
AXIAL = 128
ROW_BYTES_ROWS = CELLS * SECTIONS
STRIDE = ROWS * CELLS
PARTS = 4
PART = SECTIONS // PARTS
OWN = 40
CROSS = SECTIONS - OWN
DIRECT_CHIPS = 1
EDGE = ROW_BYTES_ROWS + SECTIONS


def device_number(region, sector, block):
    return (region * lax.axis_size("sector") + sector) * lax.axis_size("block") + block


def sector_pairs(step):
    count = lax.axis_size("sector")
    return [
        (device_number(r, s, b), device_number(r, (s + step) % count, b))
        for r in range(2)
        for s in range(count)
        for b in range(lax.axis_size("block"))
    ]


def block_pairs(first):
    count = lax.axis_size("block")
    pairs = []
    for r in range(2):
        for s in range(lax.axis_size("sector")):
            for b in range(count):
                to = b + 1 if b % 2 == first else b - 1
                if 0 <= to < count:
                    pairs.append((device_number(r, s, b), device_number(r, s, to)))
    return pairs


def turn_pairs(sectors, across):
    count = lax.axis_size("sector")
    last = lax.axis_size("block") - 1
    return [
        (
            device_number(r, s, last),
            device_number(1 - r if across else r, (s + (sectors if (r == 0) == across else -sectors)) % count, last),
        )
        for r in range(2)
        for s in range(count)
    ]


def line(index):
    return pl.ds(index * SECTIONS, SECTIONS)


def is_even(axis):
    return lax.axis_index(axis) % 2 == 0


def pack_kernel(
    shift_ref,
    field_hbm,
    speed_hbm,
    low_ref,
    high_ref,
    first_block_ref,
    second_block_ref,
    next_ref,
    prev_ref,
    first_chips_ref,
    second_chips_ref,
    field_ref,
    speed_ref,
    sems,
):
    copies = [pltpu.make_async_copy(speed_hbm, speed_ref, sems.at[PARTS])]
    for part in range(PARTS):
        where = pl.ds(part * PART * STRIDE, PART * STRIDE)
        copies.append(pltpu.make_async_copy(field_hbm.at[where, :], field_ref.at[where, :], sems.at[part]))
    for copy in copies:
        copy.start()
    for substep, chips_ref in enumerate((first_chips_ref, second_chips_ref)):
        chips = (shift_ref[substep] + CELLS) // STRIDE % (lax.axis_size("sector") // 2)
        chips_ref[...] = jnp.full((1, 1), chips, jnp.int32)
    up_is_first = is_even("block")
    for part in range(PARTS):
        copies[1 + part].wait()
        for a in range(CELLS):
            low, high = [
                field_ref[pl.ds(part * PART * STRIDE + row * CELLS + a, PART, stride=STRIDE), :] for row in range(ROWS)
            ]
            store_cells(pl.ds(a * SECTIONS + part * PART, PART), low, high, up_is_first, low_ref, high_ref, first_block_ref, second_block_ref, next_ref, prev_ref)
            if a in (0, CELLS - 1):
                edge_ref = next_ref if a else prev_ref
                edge_ref[pl.ds(ROW_BYTES_ROWS + part * PART, PART), :] = low
    copies[0].wait()
    low, high = [speed_ref[pl.ds(STRIDE + row * CELLS, CELLS), :] for row in range(ROWS)]
    first_block_ref[pl.ds(ROW_BYTES_ROWS, CELLS), :] = jnp.where(up_is_first, high, low)
    second_block_ref[pl.ds(ROW_BYTES_ROWS, CELLS), :] = jnp.where(up_is_first, low, high)
    for edge_ref, a in ((prev_ref, 0), (next_ref, CELLS - 1)):
        edge_ref[pl.ds(EDGE, 8), :] = jnp.zeros((8, AXIAL), jnp.float32)
        for row in range(ROWS):
            edge_ref[pl.ds(EDGE + row, 1), :] = speed_ref[pl.ds(row * CELLS + a, 1), :]


def store_cells(
    where, low, high, up_is_first, low_ref, high_ref, first_block_ref, second_block_ref, next_ref, prev_ref
):
    low_ref[where, :] = low
    first_block_ref[where, :] = jnp.where(up_is_first, high, low)
    second_block_ref[where, :] = jnp.where(up_is_first, low, high)
    for out_ref in (high_ref, next_ref, prev_ref):
        out_ref[where, :] = high


def lines(count):
    return jax.ShapeDtypeStruct((count, AXIAL), jnp.float32)


def vmem(count):
    return [pl.BlockSpec(memory_space=pltpu.VMEM)] * count


def pack(shifts, field, speeds):
    row = lines(ROW_BYTES_ROWS)
    rim = lines(ROW_BYTES_ROWS + CELLS)
    edge = lines(EDGE + 8)
    number = jax.ShapeDtypeStruct((1, 1), jnp.int32)
    smem = pl.BlockSpec(memory_space=pltpu.SMEM)
    return pl.pallas_call(
        pack_kernel,
        out_shape=(row, row, rim, rim, edge, edge, number, number),
        in_specs=[smem] + [pl.BlockSpec(memory_space=pltpu.HBM)] * 2,
        out_specs=tuple(vmem(8)),
        scratch_shapes=[
            pltpu.VMEM(field.shape, jnp.float32),
            pltpu.VMEM(speeds.shape, jnp.float32),
            pltpu.SemaphoreType.DMA((PARTS + 1,)),
        ],
        compiler_params=pltpu.CompilerParams(vmem_limit_bytes=GRANT),
        name="pack",
    )(shifts, field, speeds)


def align_kernel(substep, shift_ref, weight_ref, own_ref, prev_ref, next_ref, direct_ref, cross_ref, row_ref):
    @pl.when(lax.axis_index("block") == lax.axis_size("block") - 1)
    def _():
        on_stator = lax.axis_index("region") == 1
        residual = (shift_ref[substep] + CELLS) % STRIDE - CELLS
        weight = weight_ref[substep]
        for place, part_ref in enumerate((prev_ref, own_ref, next_ref)):
            row_ref[pl.ds(place * ROW_BYTES_ROWS, ROW_BYTES_ROWS), :] = part_ref[pl.ds(0, ROW_BYTES_ROWS), :]
        first = CELLS + jnp.where(on_stator, residual, -residual - 1)
        later_weight = jnp.where(on_stator, 1.0 - weight, weight)

        def cell(index):
            return row_ref[pl.ds(pl.multiple_of((first + index) * SECTIONS, SECTIONS), SECTIONS), :]

        for a in range(CELLS):
            ghost = later_weight * cell(a + 1) + (1.0 - later_weight) * cell(a)
            direct_ref[pl.ds(a * OWN, OWN), :] = ghost[:OWN]
            cross_ref[pl.ds(a * CROSS, CROSS), :] = ghost[OWN:]


def align(substep, shifts, weights, own, from_prev, from_next):
    return pl.pallas_call(
        functools.partial(align_kernel, substep),
        out_shape=(lines(CELLS * OWN), lines(CELLS * CROSS)),
        in_specs=[pl.BlockSpec(memory_space=pltpu.SMEM)] * 2 + vmem(3),
        out_specs=tuple(vmem(2)),
        scratch_shapes=[pltpu.VMEM((3 * ROW_BYTES_ROWS, AXIAL), jnp.float32)],
        compiler_params=pltpu.CompilerParams(vmem_limit_bytes=GRANT),
        name="align",
    )(shifts, weights, own, from_prev, from_next)


def split_halves(value):
    high = value.astype(jnp.bfloat16)
    low = (value - high.astype(jnp.float32)).astype(jnp.bfloat16)
    return high, low


def substep_kernel(
    final,
    low_ref,
    high_ref,
    prev_ref,
    next_ref,
    first_block_ref,
    second_block_ref,
    direct_any,
    cross_any,
    prev_rim_ref,
    next_rim_ref,
    first_block_rim_ref,
    second_block_rim_ref,
    speed_ref,
    strain_ref,
    split_ref,
    merge_ref,
    *refs,
):
    if final:
        out_any, out_ref, *scratch = refs
    else:
        new_refs, scratch = refs[:6], refs[6:]
    coef_ref, top_ref, direct_ref, cross_ref, sems = scratch
    arrivals = [
        pltpu.make_async_copy(direct_any, direct_ref, sems.at[0]),
        pltpu.make_async_copy(cross_any, cross_ref, sems.at[1]),
    ]
    for copy in arrivals:
        copy.start()
    block = lax.axis_index("block")
    first_block = block == 0
    last_block = block == lax.axis_size("block") - 1
    up_is_first = is_even("block")

    def by_block(lines_of, first_ref=first_block_ref, second_ref=second_block_ref):
        one, two = first_ref[lines_of, :], second_ref[lines_of, :]
        return jnp.where(up_is_first, one, two), jnp.where(up_is_first, two, one)

    above_speed, below_speed = by_block(pl.ds(ROW_BYTES_ROWS, CELLS), first_block_rim_ref, second_block_rim_ref)

    for row in range(ROWS):
        azim = speed_ref[pl.ds(row * CELLS, CELLS), :]
        azim_next = jnp.concatenate([azim[1:], next_rim_ref[pl.ds(EDGE + row, 1), :]], axis=0)
        azim_prev = jnp.concatenate([prev_rim_ref[pl.ds(EDGE + row, 1), :], azim[:-1]], axis=0)
        azim_high = 0.5 * (azim + azim_next)
        azim_low = 0.5 * (azim_prev + azim)
        radial = speed_ref[pl.ds(STRIDE + row * CELLS, CELLS), :]
        if row == 0:
            other = speed_ref[pl.ds(STRIDE + CELLS, CELLS), :]
            radial_high = 0.5 * (radial + other)
            radial_low = jnp.where(first_block, 0.0, 0.5 * (below_speed + radial))
        else:
            other = speed_ref[pl.ds(STRIDE, CELLS), :]
            radial_high = jnp.where(last_block, radial, 0.5 * (radial + above_speed))
            radial_low = 0.5 * (other + radial)
        axial = speed_ref[pl.ds(2 * STRIDE + row * CELLS, CELLS), :]
        axial_high = 0.5 * (axial + pltpu.roll(axial, AXIAL - 1, 1))
        axial_low = pltpu.roll(axial_high, 1, 1)
        own = 0.0
        place = row * CELLS
        for number, (high, low) in enumerate(
            ((radial_high, radial_low), (azim_high, azim_low), (axial_high, axial_low))
        ):
            own = own + jnp.maximum(high, 0.0) - jnp.minimum(low, 0.0)
            coef_ref[2 * number, pl.ds(place, CELLS), :] = -TIME_STEP * jnp.minimum(high, 0.0)
            coef_ref[2 * number + 1, pl.ds(place, CELLS), :] = TIME_STEP * jnp.maximum(low, 0.0)
        coef_ref[6, pl.ds(place, CELLS), :] = 1.0 - TIME_STEP * own
        coef_ref[7, pl.ds(place, CELLS), :] = TIME_STEP * strain_ref[pl.ds(place, CELLS), :]

    split_high, split_low = split_halves(split_ref[...])
    merge_high, merge_low = split_halves(TIME_STEP * merge_ref[...])
    both_high = jnp.concatenate([split_high, merge_high], axis=0)
    both_low = jnp.concatenate([split_low, merge_low], axis=0)
    left = jnp.concatenate([both_high, both_high, both_low], axis=1)

    leaves = []
    for row in range(ROWS):
        own_ref = (low_ref, high_ref)[row]
        if row == ROWS - 1:
            for copy in arrivals:
                copy.wait()

            @pl.when(last_block)
            def _():
                for a in range(CELLS):
                    top_ref[pl.ds(a * SECTIONS, OWN), :] = direct_ref[pl.ds(a * OWN, OWN), :]
                    top_ref[pl.ds(a * SECTIONS + OWN, CROSS), :] = cross_ref[pl.ds(a * CROSS, CROSS), :]

            @pl.when(jnp.logical_not(last_block))
            def _():
                for a in range(CELLS):
                    top_ref[line(a), :] = by_block(line(a))[0]

        for pair in range(CELLS // 2):
            cells_of = [own_ref[line(2 * pair + i), :] for i in range(2)]
            wide = jnp.concatenate(cells_of, axis=1)
            high, low = split_halves(wide)
            right = jnp.concatenate([high, low, high], axis=0)
            products = jnp.dot(left, right, preferred_element_type=jnp.float32)
            for i in range(2):
                a = 2 * pair + i
                cells = cells_of[i]
                broken = products[:SECTIONS, i * AXIAL : (i + 1) * AXIAL]
                joined = products[SECTIONS:, i * AXIAL : (i + 1) * AXIAL]
                coef = lambda n: coef_ref[n, pl.ds(row * CELLS + a, 1), :]
                if row == 0:
                    outer, inner = high_ref[line(a), :], by_block(line(a))[1]
                else:
                    outer, inner = top_ref[line(a), :], low_ref[line(a), :]
                later = next_ref[line(0 if row else CELLS), :] if a == CELLS - 1 else own_ref[line(a + 1), :]
                earlier = prev_ref[line(CELLS - 1 if row else CELLS), :] if a == 0 else own_ref[line(a - 1), :]
                value = cells * (coef(6) + joined)
                value = value + coef(7) * broken
                value = value + (coef(0) * outer + coef(1) * inner)
                value = value + (coef(2) * later + coef(3) * earlier)
                value = value + (
                    coef(4) * pltpu.roll(cells, AXIAL - 1, 1) + coef(5) * pltpu.roll(cells, 1, 1)
                )
                if final:
                    out_lines = out_ref.reshape(SECTIONS * STRIDE, AXIAL)
                    out_lines[pl.ds(row * CELLS + a, SECTIONS, stride=STRIDE), :] = value
                elif row == 0:
                    new_refs[0][line(a), :] = value
                    if a in (0, CELLS - 1):
                        edge_ref = new_refs[4] if a else new_refs[5]
                        edge_ref[line(CELLS), :] = value
                else:
                    store_cells(line(a), new_refs[0][line(a), :], value, up_is_first, *new_refs)
        if final:
            rows = pl.ds(row * CELLS, CELLS)
            leave = pltpu.make_async_copy(out_ref.at[:, rows, :], out_any.at[:, rows, :], sems.at[2 + row])
            leave.start()
            leaves.append(leave)
    for leave in leaves:
        leave.wait()


def run_substep(final, *arrays):
    scratch = [
        pltpu.VMEM((8, STRIDE, AXIAL), jnp.float32),
        pltpu.VMEM((ROW_BYTES_ROWS, AXIAL), jnp.float32),
        pltpu.VMEM((CELLS * OWN, AXIAL), jnp.float32),
        pltpu.VMEM((CELLS * CROSS, AXIAL), jnp.float32),
        pltpu.SemaphoreType.DMA((2 + ROWS,)),
    ]
    if final:
        out_shape = jax.ShapeDtypeStruct((SECTIONS, STRIDE, AXIAL), jnp.float32)
        out_specs = pl.BlockSpec(memory_space=pltpu.HBM)
        scratch.insert(0, pltpu.VMEM(out_shape.shape, jnp.float32))
    else:
        out_shape = (lines(ROW_BYTES_ROWS),) * 4 + (lines(EDGE),) * 2
        out_specs = tuple(vmem(6))
    in_specs = vmem(len(arrays))
    in_specs[6:8] = [pl.BlockSpec(memory_space=pl.ANY)] * 2
    return pl.pallas_call(
        functools.partial(substep_kernel, final),
        out_shape=out_shape,
        in_specs=in_specs,
        out_specs=out_specs,
        scratch_shapes=scratch,
        compiler_params=pltpu.CompilerParams(vmem_limit_bytes=GRANT),
        name="substep",
    )(*arrays)


def turned(chips, direct, cross):
    count = lax.axis_size("sector") // 2

    def turn(steps, direct, cross):
        distance = min(steps, count - steps)
        if distance <= DIRECT_CHIPS or 2 * distance == count:
            cross = lax.ppermute(cross, AXES, turn_pairs(2 * steps, True))
            direct = lax.ppermute(direct, AXES, turn_pairs(2 * steps, True))
        else:
            cross = lax.ppermute(cross, AXES, turn_pairs(0, True))
            direct = lax.ppermute(direct, AXES, turn_pairs(2 * steps, True))
            cross = lax.ppermute(cross, AXES, turn_pairs(2 * steps, False))
        return direct, cross

    def choose(low, high, direct, cross):
        if high - low == 1:
            return turn(low, direct, cross)
        middle = (low + high) // 2
        return lax.cond(
            chips < middle,
            functools.partial(choose, low, middle),
            functools.partial(choose, middle, high),
            direct,
            cross,
        )

    return choose(0, count, direct, cross)


def body(
    number_concentration,
    frame_motion_vector,
    strain_factor,
    splitting_kernel,
    merging_kernel,
    spinning_shift_history,
    nearest_coverage_fraction,
):
    field = number_concentration.reshape(SECTIONS * STRIDE, AXIAL)
    speeds = frame_motion_vector.reshape(3 * STRIDE, AXIAL)
    strain = strain_factor.reshape(STRIDE, AXIAL)
    shifts, weights = spinning_shift_history, nearest_coverage_fraction
    *arrays, first_chips, second_chips = pack(shifts, field, speeds)
    rims = None
    for substep, chips in enumerate((first_chips, second_chips)):
        low, high, first, second, to_next, to_prev = arrays
        from_prev = lax.ppermute(to_next, AXES, sector_pairs(1))
        from_next = lax.ppermute(to_prev, AXES, sector_pairs(-1))
        first = lax.ppermute(first, AXES, block_pairs(0))
        second = lax.ppermute(second, AXES, block_pairs(1))
        direct, cross = align(substep, shifts, weights, high, from_prev, from_next)
        direct, cross = turned(chips[0, 0], direct, cross)
        halos = (from_prev, from_next, first, second)
        rims = rims or halos
        arrays = run_substep(
            substep == 1,
            low,
            high,
            *halos,
            direct,
            cross,
            *rims,
            speeds,
            strain,
            splitting_kernel,
            merging_kernel,
        )
    return arrays.reshape(number_concentration.shape)


def solution(mesh):
    return jax.shard_map(
        body,
        mesh=mesh,
        in_specs=(
            P("region", None, "block", "sector", None),
            P("region", None, "block", "sector", None),
            P("region", "block", "sector", None),
            P(),
            P(),
            P(),
            P(),
        ),
        out_specs=P("region", None, "block", "sector", None),
        check_vma=False,
    )
```

```python
import functools

import jax
import jax.numpy as jnp
from jax import lax
from jax.experimental import pallas as pl
from jax.experimental.pallas import tpu as pltpu
from jax.sharding import PartitionSpec as P

TIME_STEP = 0.2
GRANT = 8 * 1024 * 1024
AXES = ("region", "sector", "block")
SECTIONS = 64
CELLS = 8
ROWS = 2
AXIAL = 128
ROW_BYTES_ROWS = CELLS * SECTIONS
STRIDE = ROWS * CELLS
OWN = 40
CROSS = SECTIONS - OWN
DIRECT_CHIPS = 2
EDGE = ROW_BYTES_ROWS + SECTIONS


def device_number(region, sector, block):
    return (region * lax.axis_size("sector") + sector) * lax.axis_size("block") + block


def sector_pairs(step):
    count = lax.axis_size("sector")
    return [
        (device_number(r, s, b), device_number(r, (s + step) % count, b))
        for r in range(2)
        for s in range(count)
        for b in range(lax.axis_size("block"))
    ]


def block_pairs(first):
    count = lax.axis_size("block")
    pairs = []
    for r in range(2):
        for s in range(lax.axis_size("sector")):
            for b in range(count):
                to = b + 1 if b % 2 == first else b - 1
                if 0 <= to < count:
                    pairs.append((device_number(r, s, b), device_number(r, s, to)))
    return pairs


def turn_pairs(sectors, across):
    count = lax.axis_size("sector")
    last = lax.axis_size("block") - 1
    return [
        (
            device_number(r, s, last),
            device_number(1 - r if across else r, (s + (sectors if (r == 0) == across else -sectors)) % count, last),
        )
        for r in range(2)
        for s in range(count)
    ]


def line(index):
    return pl.ds(index * SECTIONS, SECTIONS)


def is_even(axis):
    return lax.axis_index(axis) % 2 == 0


def pack_kernel(
    field_ref, speed_ref, low_ref, high_ref, first_block_ref, second_block_ref, next_ref, prev_ref
):
    up_is_first = is_even("block")
    for a in range(CELLS):
        low, high = [field_ref[pl.ds(row * CELLS + a, SECTIONS, stride=STRIDE), :] for row in range(ROWS)]
        store_cells(
            line(a), low, high, up_is_first, low_ref, high_ref, first_block_ref, second_block_ref, next_ref, prev_ref
        )
        if a in (0, CELLS - 1):
            (next_ref if a else prev_ref)[line(CELLS), :] = low
    low, high = [speed_ref[pl.ds(STRIDE + row * CELLS, CELLS), :] for row in range(ROWS)]
    first_block_ref[pl.ds(ROW_BYTES_ROWS, CELLS), :] = jnp.where(up_is_first, high, low)
    second_block_ref[pl.ds(ROW_BYTES_ROWS, CELLS), :] = jnp.where(up_is_first, low, high)
    for edge_ref, a in ((prev_ref, 0), (next_ref, CELLS - 1)):
        edge_ref[pl.ds(EDGE, 8), :] = jnp.zeros((8, AXIAL), jnp.float32)
        for row in range(ROWS):
            edge_ref[pl.ds(EDGE + row, 1), :] = speed_ref[pl.ds(row * CELLS + a, 1), :]


def store_cells(
    where, low, high, up_is_first, low_ref, high_ref, first_block_ref, second_block_ref, next_ref, prev_ref
):
    low_ref[where, :] = low
    first_block_ref[where, :] = jnp.where(up_is_first, high, low)
    second_block_ref[where, :] = jnp.where(up_is_first, low, high)
    for out_ref in (high_ref, next_ref, prev_ref):
        out_ref[where, :] = high


def lines(count):
    return jax.ShapeDtypeStruct((count, AXIAL), jnp.float32)


def vmem(count):
    return [pl.BlockSpec(memory_space=pltpu.VMEM)] * count


def pack(field, speeds):
    row = lines(ROW_BYTES_ROWS)
    rim = lines(ROW_BYTES_ROWS + CELLS)
    edge = lines(EDGE + 8)
    return pl.pallas_call(
        pack_kernel,
        out_shape=(row, row, rim, rim, edge, edge),
        in_specs=vmem(2),
        out_specs=tuple(vmem(6)),
        compiler_params=pltpu.CompilerParams(vmem_limit_bytes=GRANT),
        name="pack",
    )(field, speeds)


def align_kernel(substep, shift_ref, weight_ref, own_ref, prev_ref, next_ref, _, direct_ref, cross_ref, row_ref):
    @pl.when(lax.axis_index("block") == lax.axis_size("block") - 1)
    def _():
        on_stator = lax.axis_index("region") == 1
        chosen = lax.broadcasted_iota(jnp.int32, (1, 2), 1) == substep
        residual = (jnp.sum(jnp.where(chosen, shift_ref[...], 0)) + CELLS) % STRIDE - CELLS
        weight = jnp.sum(jnp.where(chosen, weight_ref[...], 0.0))
        for place, part_ref in enumerate((prev_ref, own_ref, next_ref)):
            row_ref[pl.ds(place * ROW_BYTES_ROWS, ROW_BYTES_ROWS), :] = part_ref[pl.ds(0, ROW_BYTES_ROWS), :]
        first = CELLS + jnp.where(on_stator, residual, -residual - 1)
        later_weight = jnp.where(on_stator, 1.0 - weight, weight)

        def cell(index):
            return row_ref[pl.ds(pl.multiple_of((first + index) * SECTIONS, SECTIONS), SECTIONS), :]

        for a in range(CELLS):
            ghost = later_weight * cell(a + 1) + (1.0 - later_weight) * cell(a)
            direct_ref[pl.ds(a * OWN, OWN), :] = ghost[:OWN]
            cross_ref[pl.ds(a * CROSS, CROSS), :] = ghost[OWN:]


def align(substep, shifts, weights, own, from_prev, from_next, strain):
    return pl.pallas_call(
        functools.partial(align_kernel, substep),
        out_shape=(lines(CELLS * OWN), lines(CELLS * CROSS)),
        in_specs=vmem(6),
        out_specs=tuple(vmem(2)),
        scratch_shapes=[pltpu.VMEM((3 * ROW_BYTES_ROWS, AXIAL), jnp.float32)],
        compiler_params=pltpu.CompilerParams(vmem_limit_bytes=GRANT),
        name="align",
    )(shifts, weights, own, from_prev, from_next, strain)


def split_halves(value):
    high = value.astype(jnp.bfloat16)
    low = (value - high.astype(jnp.float32)).astype(jnp.bfloat16)
    return high, low


def substep_kernel(
    final,
    low_ref,
    high_ref,
    prev_ref,
    next_ref,
    first_block_ref,
    second_block_ref,
    direct_any,
    cross_any,
    prev_rim_ref,
    next_rim_ref,
    first_block_rim_ref,
    second_block_rim_ref,
    speed_ref,
    strain_ref,
    split_ref,
    merge_ref,
    *refs,
):
    if final:
        out_any, out_ref, *scratch = refs
    else:
        new_refs, scratch = refs[:6], refs[6:]
    coef_ref, top_ref, direct_ref, cross_ref, sems = scratch
    arrivals = [
        pltpu.make_async_copy(direct_any, direct_ref, sems.at[0]),
        pltpu.make_async_copy(cross_any, cross_ref, sems.at[1]),
    ]
    for copy in arrivals:
        copy.start()
    block = lax.axis_index("block")
    first_block = block == 0
    last_block = block == lax.axis_size("block") - 1
    up_is_first = is_even("block")

    def by_block(lines_of, first_ref=first_block_ref, second_ref=second_block_ref):
        one, two = first_ref[lines_of, :], second_ref[lines_of, :]
        return jnp.where(up_is_first, one, two), jnp.where(up_is_first, two, one)

    above_speed, below_speed = by_block(pl.ds(ROW_BYTES_ROWS, CELLS), first_block_rim_ref, second_block_rim_ref)

    for row in range(ROWS):
        azim = speed_ref[pl.ds(row * CELLS, CELLS), :]
        azim_next = jnp.concatenate([azim[1:], next_rim_ref[pl.ds(EDGE + row, 1), :]], axis=0)
        azim_prev = jnp.concatenate([prev_rim_ref[pl.ds(EDGE + row, 1), :], azim[:-1]], axis=0)
        azim_high = 0.5 * (azim + azim_next)
        azim_low = 0.5 * (azim_prev + azim)
        radial = speed_ref[pl.ds(STRIDE + row * CELLS, CELLS), :]
        if row == 0:
            other = speed_ref[pl.ds(STRIDE + CELLS, CELLS), :]
            radial_high = 0.5 * (radial + other)
            radial_low = jnp.where(first_block, 0.0, 0.5 * (below_speed + radial))
        else:
            other = speed_ref[pl.ds(STRIDE, CELLS), :]
            radial_high = jnp.where(last_block, radial, 0.5 * (radial + above_speed))
            radial_low = 0.5 * (other + radial)
        axial = speed_ref[pl.ds(2 * STRIDE + row * CELLS, CELLS), :]
        axial_high = 0.5 * (axial + pltpu.roll(axial, AXIAL - 1, 1))
        axial_low = pltpu.roll(axial_high, 1, 1)
        own = 0.0
        place = row * CELLS
        for number, (high, low) in enumerate(
            ((radial_high, radial_low), (azim_high, azim_low), (axial_high, axial_low))
        ):
            own = own + jnp.maximum(high, 0.0) - jnp.minimum(low, 0.0)
            coef_ref[2 * number, pl.ds(place, CELLS), :] = -TIME_STEP * jnp.minimum(high, 0.0)
            coef_ref[2 * number + 1, pl.ds(place, CELLS), :] = TIME_STEP * jnp.maximum(low, 0.0)
        coef_ref[6, pl.ds(place, CELLS), :] = 1.0 - TIME_STEP * own
        coef_ref[7, pl.ds(place, CELLS), :] = TIME_STEP * strain_ref[pl.ds(place, CELLS), :]

    split_high, split_low = split_halves(split_ref[...])
    merge_high, merge_low = split_halves(TIME_STEP * merge_ref[...])
    both_high = jnp.concatenate([split_high, merge_high], axis=0)
    both_low = jnp.concatenate([split_low, merge_low], axis=0)
    left = jnp.concatenate([both_high, both_high, both_low], axis=1)

    leaves = []
    for row in range(ROWS):
        own_ref = (low_ref, high_ref)[row]
        if row == ROWS - 1:
            for copy in arrivals:
                copy.wait()

            @pl.when(last_block)
            def _():
                for a in range(CELLS):
                    top_ref[pl.ds(a * SECTIONS, OWN), :] = direct_ref[pl.ds(a * OWN, OWN), :]
                    top_ref[pl.ds(a * SECTIONS + OWN, CROSS), :] = cross_ref[pl.ds(a * CROSS, CROSS), :]

            @pl.when(jnp.logical_not(last_block))
            def _():
                for a in range(CELLS):
                    top_ref[line(a), :] = by_block(line(a))[0]

        for pair in range(CELLS // 2):
            cells_of = [own_ref[line(2 * pair + i), :] for i in range(2)]
            wide = jnp.concatenate(cells_of, axis=1)
            high, low = split_halves(wide)
            right = jnp.concatenate([high, low, high], axis=0)
            products = jnp.dot(left, right, preferred_element_type=jnp.float32)
            for i in range(2):
                a = 2 * pair + i
                cells = cells_of[i]
                broken = products[:SECTIONS, i * AXIAL : (i + 1) * AXIAL]
                joined = products[SECTIONS:, i * AXIAL : (i + 1) * AXIAL]
                coef = lambda n: coef_ref[n, pl.ds(row * CELLS + a, 1), :]
                if row == 0:
                    outer, inner = high_ref[line(a), :], by_block(line(a))[1]
                else:
                    outer, inner = top_ref[line(a), :], low_ref[line(a), :]
                later = next_ref[line(0 if row else CELLS), :] if a == CELLS - 1 else own_ref[line(a + 1), :]
                earlier = prev_ref[line(CELLS - 1 if row else CELLS), :] if a == 0 else own_ref[line(a - 1), :]
                value = cells * (coef(6) + joined)
                value = value + coef(7) * broken
                value = value + (coef(0) * outer + coef(1) * inner)
                value = value + (coef(2) * later + coef(3) * earlier)
                value = value + (
                    coef(4) * pltpu.roll(cells, AXIAL - 1, 1) + coef(5) * pltpu.roll(cells, 1, 1)
                )
                if final:
                    out_lines = out_ref.reshape(SECTIONS * STRIDE, AXIAL)
                    out_lines[pl.ds(row * CELLS + a, SECTIONS, stride=STRIDE), :] = value
                elif row == 0:
                    new_refs[0][line(a), :] = value
                    if a in (0, CELLS - 1):
                        edge_ref = new_refs[4] if a else new_refs[5]
                        edge_ref[line(CELLS), :] = value
                else:
                    store_cells(line(a), new_refs[0][line(a), :], value, up_is_first, *new_refs)
        if final:
            rows = pl.ds(row * CELLS, CELLS)
            leave = pltpu.make_async_copy(out_ref.at[:, rows, :], out_any.at[:, rows, :], sems.at[2 + row])
            leave.start()
            leaves.append(leave)
    for leave in leaves:
        leave.wait()


def run_substep(final, *arrays):
    scratch = [
        pltpu.VMEM((8, STRIDE, AXIAL), jnp.float32),
        pltpu.VMEM((ROW_BYTES_ROWS, AXIAL), jnp.float32),
        pltpu.VMEM((CELLS * OWN, AXIAL), jnp.float32),
        pltpu.VMEM((CELLS * CROSS, AXIAL), jnp.float32),
        pltpu.SemaphoreType.DMA((2 + ROWS,)),
    ]
    if final:
        out_shape = jax.ShapeDtypeStruct((SECTIONS, STRIDE, AXIAL), jnp.float32)
        out_specs = pl.BlockSpec(memory_space=pltpu.HBM)
        scratch.insert(0, pltpu.VMEM(out_shape.shape, jnp.float32))
    else:
        out_shape = (lines(ROW_BYTES_ROWS),) * 4 + (lines(EDGE),) * 2
        out_specs = tuple(vmem(6))
    in_specs = vmem(len(arrays))
    in_specs[6:8] = [pl.BlockSpec(memory_space=pl.ANY)] * 2
    return pl.pallas_call(
        functools.partial(substep_kernel, final),
        out_shape=out_shape,
        in_specs=in_specs,
        out_specs=out_specs,
        scratch_shapes=scratch,
        compiler_params=pltpu.CompilerParams(vmem_limit_bytes=GRANT),
        name="substep",
    )(*arrays)


def turned(chips, direct, cross):
    count = lax.axis_size("sector") // 2

    def turn(steps, direct, cross):
        distance = min(steps, count - steps)
        if distance <= DIRECT_CHIPS or 2 * distance == count:
            cross = lax.ppermute(cross, AXES, turn_pairs(2 * steps, True))
            direct = lax.ppermute(direct, AXES, turn_pairs(2 * steps, True))
        else:
            cross = lax.ppermute(cross, AXES, turn_pairs(0, True))
            direct = lax.ppermute(direct, AXES, turn_pairs(2 * steps, True))
            cross = lax.ppermute(cross, AXES, turn_pairs(2 * steps, False))
        return direct, cross

    def choose(low, high, direct, cross):
        if high - low == 1:
            return turn(low, direct, cross)
        middle = (low + high) // 2
        return lax.cond(
            chips < middle,
            functools.partial(choose, low, middle),
            functools.partial(choose, middle, high),
            direct,
            cross,
        )

    return choose(0, count, direct, cross)


def body(
    number_concentration,
    frame_motion_vector,
    strain_factor,
    splitting_kernel,
    merging_kernel,
    spinning_shift_history,
    nearest_coverage_fraction,
):
    field = number_concentration.reshape(SECTIONS * STRIDE, AXIAL)
    speeds = frame_motion_vector.reshape(3 * STRIDE, AXIAL)
    strain = strain_factor.reshape(STRIDE, AXIAL)
    shifts, weights = spinning_shift_history, nearest_coverage_fraction.reshape(1, 2)
    arrays = pack(field, speeds)
    rims = None
    chips = lax.rem(lax.div(shifts + CELLS, STRIDE), lax.axis_size("sector") // 2)
    turns = lax.optimization_barrier((chips, lax.rev(chips, (0,))))
    for substep in range(2):
        low, high, first, second, to_next, to_prev = arrays
        from_prev = lax.ppermute(to_next, AXES, sector_pairs(1))
        from_next = lax.ppermute(to_prev, AXES, sector_pairs(-1))
        first = lax.ppermute(first, AXES, block_pairs(0))
        second = lax.ppermute(second, AXES, block_pairs(1))
        direct, cross = align(substep, shifts.reshape(1, 2), weights, high, from_prev, from_next, strain)
        direct, cross = turned(turns[substep][0], direct, cross)
        halos = (from_prev, from_next, first, second)
        rims = rims or halos
        arrays = run_substep(
            substep == 1,
            low,
            high,
            *halos,
            direct,
            cross,
            *rims,
            speeds,
            strain,
            splitting_kernel,
            merging_kernel,
        )
    return arrays.reshape(number_concentration.shape)


def solution(mesh):
    return jax.shard_map(
        body,
        mesh=mesh,
        in_specs=(
            P("region", None, "block", "sector", None),
            P("region", None, "block", "sector", None),
            P("region", "block", "sector", None),
            P(),
            P(),
            P(),
            P(),
        ),
        out_specs=P("region", None, "block", "sector", None),
        check_vma=False,
    )
```

```python
import functools

import jax
import jax.numpy as jnp
from jax import lax
from jax.experimental import pallas as pl
from jax.experimental.pallas import tpu as pltpu
from jax.sharding import PartitionSpec as P

TIME_STEP = 0.2
GRANT = 8 * 1024 * 1024
AXES = ("region", "sector", "block")
SECTIONS = 64
CELLS = 8
ROWS = 2
AXIAL = 128
ROW_BYTES_ROWS = CELLS * SECTIONS
STRIDE = ROWS * CELLS
OWN = 40
CROSS = SECTIONS - OWN
DIRECT_CHIPS = 1
EDGE = ROW_BYTES_ROWS + SECTIONS


def device_number(region, sector, block):
    return (region * lax.axis_size("sector") + sector) * lax.axis_size("block") + block


def sector_pairs(step):
    count = lax.axis_size("sector")
    return [
        (device_number(r, s, b), device_number(r, (s + step) % count, b))
        for r in range(2)
        for s in range(count)
        for b in range(lax.axis_size("block"))
    ]


def block_pairs(first):
    count = lax.axis_size("block")
    pairs = []
    for r in range(2):
        for s in range(lax.axis_size("sector")):
            for b in range(count):
                to = b + 1 if b % 2 == first else b - 1
                if 0 <= to < count:
                    pairs.append((device_number(r, s, b), device_number(r, s, to)))
    return pairs


def turn_pairs(sectors, across):
    count = lax.axis_size("sector")
    last = lax.axis_size("block") - 1
    return [
        (
            device_number(r, s, last),
            device_number(1 - r if across else r, (s + (sectors if (r == 0) == across else -sectors)) % count, last),
        )
        for r in range(2)
        for s in range(count)
    ]


def line(index):
    return pl.ds(index * SECTIONS, SECTIONS)


def is_even(axis):
    return lax.axis_index(axis) % 2 == 0


def pack_kernel(
    field_ref, speed_ref, low_ref, high_ref, first_block_ref, second_block_ref, next_ref, prev_ref
):
    up_is_first = is_even("block")
    for a in range(CELLS):
        low, high = [field_ref[pl.ds(row * CELLS + a, SECTIONS, stride=STRIDE), :] for row in range(ROWS)]
        store_cells(
            line(a), low, high, up_is_first, low_ref, high_ref, first_block_ref, second_block_ref, next_ref, prev_ref
        )
        if a in (0, CELLS - 1):
            (next_ref if a else prev_ref)[line(CELLS), :] = low
    low, high = [speed_ref[pl.ds(STRIDE + row * CELLS, CELLS), :] for row in range(ROWS)]
    first_block_ref[pl.ds(ROW_BYTES_ROWS, CELLS), :] = jnp.where(up_is_first, high, low)
    second_block_ref[pl.ds(ROW_BYTES_ROWS, CELLS), :] = jnp.where(up_is_first, low, high)
    for edge_ref, a in ((prev_ref, 0), (next_ref, CELLS - 1)):
        edge_ref[pl.ds(EDGE, 8), :] = jnp.zeros((8, AXIAL), jnp.float32)
        for row in range(ROWS):
            edge_ref[pl.ds(EDGE + row, 1), :] = speed_ref[pl.ds(row * CELLS + a, 1), :]


def store_cells(
    where, low, high, up_is_first, low_ref, high_ref, first_block_ref, second_block_ref, next_ref, prev_ref
):
    low_ref[where, :] = low
    first_block_ref[where, :] = jnp.where(up_is_first, high, low)
    second_block_ref[where, :] = jnp.where(up_is_first, low, high)
    for out_ref in (high_ref, next_ref, prev_ref):
        out_ref[where, :] = high


def lines(count):
    return jax.ShapeDtypeStruct((count, AXIAL), jnp.float32)


def vmem(count):
    return [pl.BlockSpec(memory_space=pltpu.VMEM)] * count


def pack(field, speeds):
    row = lines(ROW_BYTES_ROWS)
    rim = lines(ROW_BYTES_ROWS + CELLS)
    edge = lines(EDGE + 8)
    return pl.pallas_call(
        pack_kernel,
        out_shape=(row, row, rim, rim, edge, edge),
        in_specs=vmem(2),
        out_specs=tuple(vmem(6)),
        compiler_params=pltpu.CompilerParams(vmem_limit_bytes=GRANT),
        name="pack",
    )(field, speeds)


def align_kernel(substep, shift_ref, weight_ref, own_ref, prev_ref, next_ref, _, direct_ref, cross_ref, row_ref):
    @pl.when(lax.axis_index("block") == lax.axis_size("block") - 1)
    def _():
        on_stator = lax.axis_index("region") == 1
        chosen = lax.broadcasted_iota(jnp.int32, (1, 2), 1) == substep
        residual = (jnp.sum(jnp.where(chosen, shift_ref[...], 0)) + CELLS) % STRIDE - CELLS
        weight = jnp.sum(jnp.where(chosen, weight_ref[...], 0.0))
        for place, part_ref in enumerate((prev_ref, own_ref, next_ref)):
            row_ref[pl.ds(place * ROW_BYTES_ROWS, ROW_BYTES_ROWS), :] = part_ref[pl.ds(0, ROW_BYTES_ROWS), :]
        first = CELLS + jnp.where(on_stator, residual, -residual - 1)
        later_weight = jnp.where(on_stator, 1.0 - weight, weight)

        def cell(index):
            return row_ref[pl.ds(pl.multiple_of((first + index) * SECTIONS, SECTIONS), SECTIONS), :]

        for a in range(CELLS):
            ghost = later_weight * cell(a + 1) + (1.0 - later_weight) * cell(a)
            direct_ref[pl.ds(a * OWN, OWN), :] = ghost[:OWN]
            cross_ref[pl.ds(a * CROSS, CROSS), :] = ghost[OWN:]


def align(substep, shifts, weights, own, from_prev, from_next, strain):
    return pl.pallas_call(
        functools.partial(align_kernel, substep),
        out_shape=(lines(CELLS * OWN), lines(CELLS * CROSS)),
        in_specs=vmem(6),
        out_specs=tuple(vmem(2)),
        scratch_shapes=[pltpu.VMEM((3 * ROW_BYTES_ROWS, AXIAL), jnp.float32)],
        compiler_params=pltpu.CompilerParams(vmem_limit_bytes=GRANT),
        name="align",
    )(shifts, weights, own, from_prev, from_next, strain)


def split_halves(value):
    high = value.astype(jnp.bfloat16)
    low = (value - high.astype(jnp.float32)).astype(jnp.bfloat16)
    return high, low


def substep_kernel(
    final,
    low_ref,
    high_ref,
    prev_ref,
    next_ref,
    first_block_ref,
    second_block_ref,
    direct_any,
    cross_any,
    prev_rim_ref,
    next_rim_ref,
    first_block_rim_ref,
    second_block_rim_ref,
    speed_ref,
    strain_ref,
    split_ref,
    merge_ref,
    *refs,
):
    if final:
        out_any, out_ref, *scratch = refs
    else:
        new_refs, scratch = refs[:6], refs[6:]
    coef_ref, top_ref, direct_ref, cross_ref, sems = scratch
    arrivals = [
        pltpu.make_async_copy(direct_any, direct_ref, sems.at[0]),
        pltpu.make_async_copy(cross_any, cross_ref, sems.at[1]),
    ]
    for copy in arrivals:
        copy.start()
    block = lax.axis_index("block")
    first_block = block == 0
    last_block = block == lax.axis_size("block") - 1
    up_is_first = is_even("block")

    def by_block(lines_of, first_ref=first_block_ref, second_ref=second_block_ref):
        one, two = first_ref[lines_of, :], second_ref[lines_of, :]
        return jnp.where(up_is_first, one, two), jnp.where(up_is_first, two, one)

    above_speed, below_speed = by_block(pl.ds(ROW_BYTES_ROWS, CELLS), first_block_rim_ref, second_block_rim_ref)

    for row in range(ROWS):
        azim = speed_ref[pl.ds(row * CELLS, CELLS), :]
        azim_next = jnp.concatenate([azim[1:], next_rim_ref[pl.ds(EDGE + row, 1), :]], axis=0)
        azim_prev = jnp.concatenate([prev_rim_ref[pl.ds(EDGE + row, 1), :], azim[:-1]], axis=0)
        azim_high = 0.5 * (azim + azim_next)
        azim_low = 0.5 * (azim_prev + azim)
        radial = speed_ref[pl.ds(STRIDE + row * CELLS, CELLS), :]
        if row == 0:
            other = speed_ref[pl.ds(STRIDE + CELLS, CELLS), :]
            radial_high = 0.5 * (radial + other)
            radial_low = jnp.where(first_block, 0.0, 0.5 * (below_speed + radial))
        else:
            other = speed_ref[pl.ds(STRIDE, CELLS), :]
            radial_high = jnp.where(last_block, radial, 0.5 * (radial + above_speed))
            radial_low = 0.5 * (other + radial)
        axial = speed_ref[pl.ds(2 * STRIDE + row * CELLS, CELLS), :]
        axial_high = 0.5 * (axial + pltpu.roll(axial, AXIAL - 1, 1))
        axial_low = pltpu.roll(axial_high, 1, 1)
        own = 0.0
        place = row * CELLS
        for number, (high, low) in enumerate(
            ((radial_high, radial_low), (azim_high, azim_low), (axial_high, axial_low))
        ):
            own = own + jnp.maximum(high, 0.0) - jnp.minimum(low, 0.0)
            coef_ref[2 * number, pl.ds(place, CELLS), :] = -TIME_STEP * jnp.minimum(high, 0.0)
            coef_ref[2 * number + 1, pl.ds(place, CELLS), :] = TIME_STEP * jnp.maximum(low, 0.0)
        coef_ref[6, pl.ds(place, CELLS), :] = 1.0 - TIME_STEP * own
        coef_ref[7, pl.ds(place, CELLS), :] = TIME_STEP * strain_ref[pl.ds(place, CELLS), :]

    split_high, split_low = split_halves(split_ref[...])
    merge_high, merge_low = split_halves(TIME_STEP * merge_ref[...])
    both_high = jnp.concatenate([split_high, merge_high], axis=0)
    both_low = jnp.concatenate([split_low, merge_low], axis=0)
    left = jnp.concatenate([both_high, both_high, both_low], axis=1)

    leaves = []
    for row in range(ROWS):
        own_ref = (low_ref, high_ref)[row]
        if row == ROWS - 1:
            for copy in arrivals:
                copy.wait()

            @pl.when(last_block)
            def _():
                for a in range(CELLS):
                    top_ref[pl.ds(a * SECTIONS, OWN), :] = direct_ref[pl.ds(a * OWN, OWN), :]
                    top_ref[pl.ds(a * SECTIONS + OWN, CROSS), :] = cross_ref[pl.ds(a * CROSS, CROSS), :]

            @pl.when(jnp.logical_not(last_block))
            def _():
                for a in range(CELLS):
                    top_ref[line(a), :] = by_block(line(a))[0]

        for pair in range(CELLS // 2):
            cells_of = [own_ref[line(2 * pair + i), :] for i in range(2)]
            wide = jnp.concatenate(cells_of, axis=1)
            high, low = split_halves(wide)
            right = jnp.concatenate([high, low, high], axis=0)
            products = jnp.dot(left, right, preferred_element_type=jnp.float32)
            for i in range(2):
                a = 2 * pair + i
                cells = cells_of[i]
                broken = products[:SECTIONS, i * AXIAL : (i + 1) * AXIAL]
                joined = products[SECTIONS:, i * AXIAL : (i + 1) * AXIAL]
                coef = lambda n: coef_ref[n, pl.ds(row * CELLS + a, 1), :]
                if row == 0:
                    outer, inner = high_ref[line(a), :], by_block(line(a))[1]
                else:
                    outer, inner = top_ref[line(a), :], low_ref[line(a), :]
                later = next_ref[line(0 if row else CELLS), :] if a == CELLS - 1 else own_ref[line(a + 1), :]
                earlier = prev_ref[line(CELLS - 1 if row else CELLS), :] if a == 0 else own_ref[line(a - 1), :]
                value = cells * (coef(6) + joined)
                value = value + coef(7) * broken
                value = value + (coef(0) * outer + coef(1) * inner)
                value = value + (coef(2) * later + coef(3) * earlier)
                value = value + (
                    coef(4) * pltpu.roll(cells, AXIAL - 1, 1) + coef(5) * pltpu.roll(cells, 1, 1)
                )
                if final:
                    out_lines = out_ref.reshape(SECTIONS * STRIDE, AXIAL)
                    out_lines[pl.ds(row * CELLS + a, SECTIONS, stride=STRIDE), :] = value
                elif row == 0:
                    new_refs[0][line(a), :] = value
                    if a in (0, CELLS - 1):
                        edge_ref = new_refs[4] if a else new_refs[5]
                        edge_ref[line(CELLS), :] = value
                else:
                    store_cells(line(a), new_refs[0][line(a), :], value, up_is_first, *new_refs)
        if final:
            rows = pl.ds(row * CELLS, CELLS)
            leave = pltpu.make_async_copy(out_ref.at[:, rows, :], out_any.at[:, rows, :], sems.at[2 + row])
            leave.start()
            leaves.append(leave)
    for leave in leaves:
        leave.wait()


def run_substep(final, *arrays):
    scratch = [
        pltpu.VMEM((8, STRIDE, AXIAL), jnp.float32),
        pltpu.VMEM((ROW_BYTES_ROWS, AXIAL), jnp.float32),
        pltpu.VMEM((CELLS * OWN, AXIAL), jnp.float32),
        pltpu.VMEM((CELLS * CROSS, AXIAL), jnp.float32),
        pltpu.SemaphoreType.DMA((2 + ROWS,)),
    ]
    if final:
        out_shape = jax.ShapeDtypeStruct((SECTIONS, STRIDE, AXIAL), jnp.float32)
        out_specs = pl.BlockSpec(memory_space=pltpu.HBM)
        scratch.insert(0, pltpu.VMEM(out_shape.shape, jnp.float32))
    else:
        out_shape = (lines(ROW_BYTES_ROWS),) * 4 + (lines(EDGE),) * 2
        out_specs = tuple(vmem(6))
    in_specs = vmem(len(arrays))
    in_specs[6:8] = [pl.BlockSpec(memory_space=pl.ANY)] * 2
    return pl.pallas_call(
        functools.partial(substep_kernel, final),
        out_shape=out_shape,
        in_specs=in_specs,
        out_specs=out_specs,
        scratch_shapes=scratch,
        compiler_params=pltpu.CompilerParams(vmem_limit_bytes=GRANT),
        name="substep",
    )(*arrays)


def turned(chips, direct, cross):
    count = lax.axis_size("sector") // 2

    def turn(steps, direct, cross):
        distance = min(steps, count - steps)
        if distance <= DIRECT_CHIPS or 2 * distance == count:
            cross = lax.ppermute(cross, AXES, turn_pairs(2 * steps, True))
            direct = lax.ppermute(direct, AXES, turn_pairs(2 * steps, True))
        else:
            cross = lax.ppermute(cross, AXES, turn_pairs(0, True))
            direct = lax.ppermute(direct, AXES, turn_pairs(2 * steps, True))
            cross = lax.ppermute(cross, AXES, turn_pairs(2 * steps, False))
        return direct, cross

    return lax.switch(chips, [functools.partial(turn, steps) for steps in range(count)], direct, cross)


def body(
    number_concentration,
    frame_motion_vector,
    strain_factor,
    splitting_kernel,
    merging_kernel,
    spinning_shift_history,
    nearest_coverage_fraction,
):
    field = number_concentration.reshape(SECTIONS * STRIDE, AXIAL)
    speeds = frame_motion_vector.reshape(3 * STRIDE, AXIAL)
    strain = strain_factor.reshape(STRIDE, AXIAL)
    shifts, weights = spinning_shift_history, nearest_coverage_fraction.reshape(1, 2)
    arrays = pack(field, speeds)
    rims = None
    chips = lax.rem(lax.div(shifts + CELLS, STRIDE), lax.axis_size("sector") // 2)
    turns = lax.optimization_barrier((chips, lax.rev(chips, (0,))))
    for substep in range(2):
        low, high, first, second, to_next, to_prev = arrays
        from_prev = lax.ppermute(to_next, AXES, sector_pairs(1))
        from_next = lax.ppermute(to_prev, AXES, sector_pairs(-1))
        first = lax.ppermute(first, AXES, block_pairs(0))
        second = lax.ppermute(second, AXES, block_pairs(1))
        direct, cross = align(substep, shifts.reshape(1, 2), weights, high, from_prev, from_next, strain)
        direct, cross = turned(turns[substep][0], direct, cross)
        halos = (from_prev, from_next, first, second)
        rims = rims or halos
        arrays = run_substep(
            substep == 1,
            low,
            high,
            *halos,
            direct,
            cross,
            *rims,
            speeds,
            strain,
            splitting_kernel,
            merging_kernel,
        )
    return arrays.reshape(number_concentration.shape)


def solution(mesh):
    return jax.shard_map(
        body,
        mesh=mesh,
        in_specs=(
            P("region", None, "block", "sector", None),
            P("region", None, "block", "sector", None),
            P("region", "block", "sector", None),
            P(),
            P(),
            P(),
            P(),
        ),
        out_specs=P("region", None, "block", "sector", None),
        check_vma=False,
    )
```

```python
import functools

import jax
import jax.numpy as jnp
from jax import lax
from jax.experimental import pallas as pl
from jax.experimental.pallas import tpu as pltpu
from jax.sharding import PartitionSpec as P

TIME_STEP = 0.2
GRANT = 8 * 1024 * 1024
AXES = ("region", "sector", "block")
SECTIONS = 64
CELLS = 8
ROWS = 2
AXIAL = 128
ROW_BYTES_ROWS = CELLS * SECTIONS
STRIDE = ROWS * CELLS
OWN = 40
CROSS = SECTIONS - OWN
DIRECT_CHIPS = 2
EDGE = ROW_BYTES_ROWS + SECTIONS


def device_number(region, sector, block):
    return (region * lax.axis_size("sector") + sector) * lax.axis_size("block") + block


def sector_pairs(step):
    count = lax.axis_size("sector")
    return [
        (device_number(r, s, b), device_number(r, (s + step) % count, b))
        for r in range(2)
        for s in range(count)
        for b in range(lax.axis_size("block"))
    ]


def block_pairs(first):
    count = lax.axis_size("block")
    pairs = []
    for r in range(2):
        for s in range(lax.axis_size("sector")):
            for b in range(count):
                to = b + 1 if b % 2 == first else b - 1
                if 0 <= to < count:
                    pairs.append((device_number(r, s, b), device_number(r, s, to)))
    return pairs


def turn_pairs(sectors, across):
    count = lax.axis_size("sector")
    last = lax.axis_size("block") - 1
    return [
        (
            device_number(r, s, last),
            device_number(1 - r if across else r, (s + (sectors if (r == 0) == across else -sectors)) % count, last),
        )
        for r in range(2)
        for s in range(count)
    ]


def line(index):
    return pl.ds(index * SECTIONS, SECTIONS)


def is_even(axis):
    return lax.axis_index(axis) % 2 == 0


def pack_kernel(
    field_ref, speed_ref, low_ref, high_ref, first_block_ref, second_block_ref, next_ref, prev_ref
):
    up_is_first = is_even("block")
    for a in range(CELLS):
        low, high = [field_ref[pl.ds(row * CELLS + a, SECTIONS, stride=STRIDE), :] for row in range(ROWS)]
        store_cells(
            line(a), low, high, up_is_first, low_ref, high_ref, first_block_ref, second_block_ref, next_ref, prev_ref
        )
        if a in (0, CELLS - 1):
            (next_ref if a else prev_ref)[line(CELLS), :] = low
    low, high = [speed_ref[pl.ds(STRIDE + row * CELLS, CELLS), :] for row in range(ROWS)]
    first_block_ref[pl.ds(ROW_BYTES_ROWS, CELLS), :] = jnp.where(up_is_first, high, low)
    second_block_ref[pl.ds(ROW_BYTES_ROWS, CELLS), :] = jnp.where(up_is_first, low, high)
    for edge_ref, a in ((prev_ref, 0), (next_ref, CELLS - 1)):
        edge_ref[pl.ds(EDGE, 8), :] = jnp.zeros((8, AXIAL), jnp.float32)
        for row in range(ROWS):
            edge_ref[pl.ds(EDGE + row, 1), :] = speed_ref[pl.ds(row * CELLS + a, 1), :]


def store_cells(
    where, low, high, up_is_first, low_ref, high_ref, first_block_ref, second_block_ref, next_ref, prev_ref
):
    low_ref[where, :] = low
    first_block_ref[where, :] = jnp.where(up_is_first, high, low)
    second_block_ref[where, :] = jnp.where(up_is_first, low, high)
    for out_ref in (high_ref, next_ref, prev_ref):
        out_ref[where, :] = high


def lines(count):
    return jax.ShapeDtypeStruct((count, AXIAL), jnp.float32)


def vmem(count):
    return [pl.BlockSpec(memory_space=pltpu.VMEM)] * count


def pack(field, speeds):
    row = lines(ROW_BYTES_ROWS)
    rim = lines(ROW_BYTES_ROWS + CELLS)
    edge = lines(EDGE + 8)
    return pl.pallas_call(
        pack_kernel,
        out_shape=(row, row, rim, rim, edge, edge),
        in_specs=vmem(2),
        out_specs=tuple(vmem(6)),
        compiler_params=pltpu.CompilerParams(vmem_limit_bytes=GRANT),
        name="pack",
    )(field, speeds)


def align_kernel(substep, shift_ref, weight_ref, own_ref, prev_ref, next_ref, _, direct_ref, cross_ref, row_ref):
    @pl.when(lax.axis_index("block") == lax.axis_size("block") - 1)
    def _():
        on_stator = lax.axis_index("region") == 1
        chosen = lax.broadcasted_iota(jnp.int32, (1, 2), 1) == substep
        residual = (jnp.sum(jnp.where(chosen, shift_ref[...], 0)) + CELLS) % STRIDE - CELLS
        weight = jnp.sum(jnp.where(chosen, weight_ref[...], 0.0))
        for place, part_ref in enumerate((prev_ref, own_ref, next_ref)):
            row_ref[pl.ds(place * ROW_BYTES_ROWS, ROW_BYTES_ROWS), :] = part_ref[pl.ds(0, ROW_BYTES_ROWS), :]
        first = CELLS + jnp.where(on_stator, residual, -residual - 1)
        later_weight = jnp.where(on_stator, 1.0 - weight, weight)

        def cell(index):
            return row_ref[pl.ds(pl.multiple_of((first + index) * SECTIONS, SECTIONS), SECTIONS), :]

        for a in range(CELLS):
            ghost = later_weight * cell(a + 1) + (1.0 - later_weight) * cell(a)
            direct_ref[pl.ds(a * OWN, OWN), :] = ghost[:OWN]
            cross_ref[pl.ds(a * CROSS, CROSS), :] = ghost[OWN:]


def align(substep, shifts, weights, own, from_prev, from_next, strain):
    return pl.pallas_call(
        functools.partial(align_kernel, substep),
        out_shape=(lines(CELLS * OWN), lines(CELLS * CROSS)),
        in_specs=vmem(6),
        out_specs=tuple(vmem(2)),
        scratch_shapes=[pltpu.VMEM((3 * ROW_BYTES_ROWS, AXIAL), jnp.float32)],
        compiler_params=pltpu.CompilerParams(vmem_limit_bytes=GRANT),
        name="align",
    )(shifts, weights, own, from_prev, from_next, strain)


def split_halves(value):
    high = value.astype(jnp.bfloat16)
    low = (value - high.astype(jnp.float32)).astype(jnp.bfloat16)
    return high, low


def substep_kernel(
    final,
    low_ref,
    high_ref,
    prev_ref,
    next_ref,
    first_block_ref,
    second_block_ref,
    direct_any,
    cross_any,
    prev_rim_ref,
    next_rim_ref,
    first_block_rim_ref,
    second_block_rim_ref,
    speed_ref,
    strain_ref,
    split_ref,
    merge_ref,
    *refs,
):
    if final:
        out_any, out_ref, *scratch = refs
    else:
        new_refs, scratch = refs[:6], refs[6:]
    coef_ref, top_ref, direct_ref, cross_ref, sems = scratch
    arrivals = [
        pltpu.make_async_copy(direct_any, direct_ref, sems.at[0]),
        pltpu.make_async_copy(cross_any, cross_ref, sems.at[1]),
    ]
    for copy in arrivals:
        copy.start()
    block = lax.axis_index("block")
    first_block = block == 0
    last_block = block == lax.axis_size("block") - 1
    up_is_first = is_even("block")

    def by_block(lines_of, first_ref=first_block_ref, second_ref=second_block_ref):
        one, two = first_ref[lines_of, :], second_ref[lines_of, :]
        return jnp.where(up_is_first, one, two), jnp.where(up_is_first, two, one)

    above_speed, below_speed = by_block(pl.ds(ROW_BYTES_ROWS, CELLS), first_block_rim_ref, second_block_rim_ref)

    for row in range(ROWS):
        azim = speed_ref[pl.ds(row * CELLS, CELLS), :]
        azim_next = jnp.concatenate([azim[1:], next_rim_ref[pl.ds(EDGE + row, 1), :]], axis=0)
        azim_prev = jnp.concatenate([prev_rim_ref[pl.ds(EDGE + row, 1), :], azim[:-1]], axis=0)
        azim_high = 0.5 * (azim + azim_next)
        azim_low = 0.5 * (azim_prev + azim)
        radial = speed_ref[pl.ds(STRIDE + row * CELLS, CELLS), :]
        if row == 0:
            other = speed_ref[pl.ds(STRIDE + CELLS, CELLS), :]
            radial_high = 0.5 * (radial + other)
            radial_low = jnp.where(first_block, 0.0, 0.5 * (below_speed + radial))
        else:
            other = speed_ref[pl.ds(STRIDE, CELLS), :]
            radial_high = jnp.where(last_block, radial, 0.5 * (radial + above_speed))
            radial_low = 0.5 * (other + radial)
        axial = speed_ref[pl.ds(2 * STRIDE + row * CELLS, CELLS), :]
        axial_high = 0.5 * (axial + pltpu.roll(axial, AXIAL - 1, 1))
        axial_low = pltpu.roll(axial_high, 1, 1)
        own = 0.0
        place = row * CELLS
        for number, (high, low) in enumerate(
            ((radial_high, radial_low), (azim_high, azim_low), (axial_high, axial_low))
        ):
            own = own + jnp.maximum(high, 0.0) - jnp.minimum(low, 0.0)
            coef_ref[2 * number, pl.ds(place, CELLS), :] = -TIME_STEP * jnp.minimum(high, 0.0)
            coef_ref[2 * number + 1, pl.ds(place, CELLS), :] = TIME_STEP * jnp.maximum(low, 0.0)
        coef_ref[6, pl.ds(place, CELLS), :] = 1.0 - TIME_STEP * own
        coef_ref[7, pl.ds(place, CELLS), :] = TIME_STEP * strain_ref[pl.ds(place, CELLS), :]

    split_high, split_low = split_halves(split_ref[...])
    merge_high, merge_low = split_halves(TIME_STEP * merge_ref[...])
    both_high = jnp.concatenate([split_high, merge_high], axis=0)
    both_low = jnp.concatenate([split_low, merge_low], axis=0)
    left = jnp.concatenate([both_high, both_high, both_low], axis=1)

    leaves = []
    for row in range(ROWS):
        own_ref = (low_ref, high_ref)[row]
        if row == ROWS - 1:
            for copy in arrivals:
                copy.wait()

            @pl.when(last_block)
            def _():
                for a in range(CELLS):
                    top_ref[pl.ds(a * SECTIONS, OWN), :] = direct_ref[pl.ds(a * OWN, OWN), :]
                    top_ref[pl.ds(a * SECTIONS + OWN, CROSS), :] = cross_ref[pl.ds(a * CROSS, CROSS), :]

            @pl.when(jnp.logical_not(last_block))
            def _():
                for a in range(CELLS):
                    top_ref[line(a), :] = by_block(line(a))[0]

        for pair in range(CELLS // 2):
            cells_of = [own_ref[line(2 * pair + i), :] for i in range(2)]
            wide = jnp.concatenate(cells_of, axis=1)
            high, low = split_halves(wide)
            right = jnp.concatenate([high, low, high], axis=0)
            products = jnp.dot(left, right, preferred_element_type=jnp.float32)
            for i in range(2):
                a = 2 * pair + i
                cells = cells_of[i]
                broken = products[:SECTIONS, i * AXIAL : (i + 1) * AXIAL]
                joined = products[SECTIONS:, i * AXIAL : (i + 1) * AXIAL]
                coef = lambda n: coef_ref[n, pl.ds(row * CELLS + a, 1), :]
                if row == 0:
                    outer, inner = high_ref[line(a), :], by_block(line(a))[1]
                else:
                    outer, inner = top_ref[line(a), :], low_ref[line(a), :]
                later = next_ref[line(0 if row else CELLS), :] if a == CELLS - 1 else own_ref[line(a + 1), :]
                earlier = prev_ref[line(CELLS - 1 if row else CELLS), :] if a == 0 else own_ref[line(a - 1), :]
                value = cells * (coef(6) + joined)
                value = value + coef(7) * broken
                value = value + (coef(0) * outer + coef(1) * inner)
                value = value + (coef(2) * later + coef(3) * earlier)
                value = value + (
                    coef(4) * pltpu.roll(cells, AXIAL - 1, 1) + coef(5) * pltpu.roll(cells, 1, 1)
                )
                if final:
                    out_lines = out_ref.reshape(SECTIONS * STRIDE, AXIAL)
                    out_lines[pl.ds(row * CELLS + a, SECTIONS, stride=STRIDE), :] = value
                elif row == 0:
                    new_refs[0][line(a), :] = value
                    if a in (0, CELLS - 1):
                        edge_ref = new_refs[4] if a else new_refs[5]
                        edge_ref[line(CELLS), :] = value
                else:
                    store_cells(line(a), new_refs[0][line(a), :], value, up_is_first, *new_refs)
        if final:
            rows = pl.ds(row * CELLS, CELLS)
            leave = pltpu.make_async_copy(out_ref.at[:, rows, :], out_any.at[:, rows, :], sems.at[2 + row])
            leave.start()
            leaves.append(leave)
    for leave in leaves:
        leave.wait()


def run_substep(final, *arrays):
    scratch = [
        pltpu.VMEM((8, STRIDE, AXIAL), jnp.float32),
        pltpu.VMEM((ROW_BYTES_ROWS, AXIAL), jnp.float32),
        pltpu.VMEM((CELLS * OWN, AXIAL), jnp.float32),
        pltpu.VMEM((CELLS * CROSS, AXIAL), jnp.float32),
        pltpu.SemaphoreType.DMA((2 + ROWS,)),
    ]
    if final:
        out_shape = jax.ShapeDtypeStruct((SECTIONS, STRIDE, AXIAL), jnp.float32)
        out_specs = pl.BlockSpec(memory_space=pltpu.HBM)
        scratch.insert(0, pltpu.VMEM(out_shape.shape, jnp.float32))
    else:
        out_shape = (lines(ROW_BYTES_ROWS),) * 4 + (lines(EDGE),) * 2
        out_specs = tuple(vmem(6))
    in_specs = vmem(len(arrays))
    in_specs[6:8] = [pl.BlockSpec(memory_space=pl.ANY)] * 2
    return pl.pallas_call(
        functools.partial(substep_kernel, final),
        out_shape=out_shape,
        in_specs=in_specs,
        out_specs=out_specs,
        scratch_shapes=scratch,
        compiler_params=pltpu.CompilerParams(vmem_limit_bytes=GRANT),
        name="substep",
    )(*arrays)


def turned(chips, direct, cross):
    count = lax.axis_size("sector") // 2

    def turn(steps, direct, cross):
        distance = min(steps, count - steps)
        if distance <= DIRECT_CHIPS:
            whole = jnp.concatenate([direct, cross], axis=0)
            whole = lax.ppermute(whole, AXES, turn_pairs(2 * steps, True))
            direct, cross = whole[: CELLS * OWN], whole[CELLS * OWN :]
        elif 2 * distance == count:
            cross = lax.ppermute(cross, AXES, turn_pairs(2 * steps, True))
            direct = lax.ppermute(direct, AXES, turn_pairs(2 * steps, True))
        else:
            cross = lax.ppermute(cross, AXES, turn_pairs(0, True))
            direct = lax.ppermute(direct, AXES, turn_pairs(2 * steps, True))
            cross = lax.ppermute(cross, AXES, turn_pairs(2 * steps, False))
        return direct, cross

    return lax.switch(chips, [functools.partial(turn, steps) for steps in range(count)], direct, cross)


def body(
    number_concentration,
    frame_motion_vector,
    strain_factor,
    splitting_kernel,
    merging_kernel,
    spinning_shift_history,
    nearest_coverage_fraction,
):
    field = number_concentration.reshape(SECTIONS * STRIDE, AXIAL)
    speeds = frame_motion_vector.reshape(3 * STRIDE, AXIAL)
    strain = strain_factor.reshape(STRIDE, AXIAL)
    shifts, weights = spinning_shift_history, nearest_coverage_fraction.reshape(1, 2)
    arrays = pack(field, speeds)
    rims = None
    chips = lax.rem(lax.div(shifts + CELLS, STRIDE), lax.axis_size("sector") // 2)
    turns = lax.optimization_barrier((chips, lax.rev(chips, (0,))))
    for substep in range(2):
        low, high, first, second, to_next, to_prev = arrays
        from_prev = lax.ppermute(to_next, AXES, sector_pairs(1))
        from_next = lax.ppermute(to_prev, AXES, sector_pairs(-1))
        first = lax.ppermute(first, AXES, block_pairs(0))
        second = lax.ppermute(second, AXES, block_pairs(1))
        direct, cross = align(substep, shifts.reshape(1, 2), weights, high, from_prev, from_next, strain)
        direct, cross = turned(turns[substep][0], direct, cross)
        halos = (from_prev, from_next, first, second)
        rims = rims or halos
        arrays = run_substep(
            substep == 1,
            low,
            high,
            *halos,
            direct,
            cross,
            *rims,
            speeds,
            strain,
            splitting_kernel,
            merging_kernel,
        )
    return arrays.reshape(number_concentration.shape)


def solution(mesh):
    return jax.shard_map(
        body,
        mesh=mesh,
        in_specs=(
            P("region", None, "block", "sector", None),
            P("region", None, "block", "sector", None),
            P("region", "block", "sector", None),
            P(),
            P(),
            P(),
            P(),
        ),
        out_specs=P("region", None, "block", "sector", None),
        check_vma=False,
    )
```

```python
import functools

import jax
import jax.numpy as jnp
from jax import lax
from jax.experimental import pallas as pl
from jax.experimental.pallas import tpu as pltpu
from jax.sharding import PartitionSpec as P

TIME_STEP = 0.2
GRANT = 8 * 1024 * 1024
AXES = ("region", "sector", "block")
SECTIONS = 64
CELLS = 8
ROWS = 2
AXIAL = 128
ROW_BYTES_ROWS = CELLS * SECTIONS
STRIDE = ROWS * CELLS
OWN = 40
CROSS = SECTIONS - OWN
DIRECT_CHIPS = 1
EDGE = ROW_BYTES_ROWS + SECTIONS


def device_number(region, sector, block):
    return (region * lax.axis_size("sector") + sector) * lax.axis_size("block") + block


def sector_pairs(step):
    count = lax.axis_size("sector")
    return [
        (device_number(r, s, b), device_number(r, (s + step) % count, b))
        for r in range(2)
        for s in range(count)
        for b in range(lax.axis_size("block"))
    ]


def block_pairs(first):
    count = lax.axis_size("block")
    pairs = []
    for r in range(2):
        for s in range(lax.axis_size("sector")):
            for b in range(count):
                to = b + 1 if b % 2 == first else b - 1
                if 0 <= to < count:
                    pairs.append((device_number(r, s, b), device_number(r, s, to)))
    return pairs


def turn_pairs(sectors, across):
    count = lax.axis_size("sector")
    last = lax.axis_size("block") - 1
    return [
        (
            device_number(r, s, last),
            device_number(1 - r if across else r, (s + (sectors if (r == 0) == across else -sectors)) % count, last),
        )
        for r in range(2)
        for s in range(count)
    ]


def line(index):
    return pl.ds(index * SECTIONS, SECTIONS)


def is_even(axis):
    return lax.axis_index(axis) % 2 == 0


def pack_kernel(
    field_ref, speed_ref, low_ref, high_ref, first_block_ref, second_block_ref, next_ref, prev_ref
):
    up_is_first = is_even("block")
    for a in range(CELLS):
        low, high = [field_ref[pl.ds(row * CELLS + a, SECTIONS, stride=STRIDE), :] for row in range(ROWS)]
        store_cells(
            line(a), low, high, up_is_first, low_ref, high_ref, first_block_ref, second_block_ref, next_ref, prev_ref
        )
        if a in (0, CELLS - 1):
            (next_ref if a else prev_ref)[line(CELLS), :] = low
    low, high = [speed_ref[pl.ds(STRIDE + row * CELLS, CELLS), :] for row in range(ROWS)]
    first_block_ref[pl.ds(ROW_BYTES_ROWS, CELLS), :] = jnp.where(up_is_first, high, low)
    second_block_ref[pl.ds(ROW_BYTES_ROWS, CELLS), :] = jnp.where(up_is_first, low, high)
    for edge_ref, a in ((prev_ref, 0), (next_ref, CELLS - 1)):
        edge_ref[pl.ds(EDGE, 8), :] = jnp.zeros((8, AXIAL), jnp.float32)
        for row in range(ROWS):
            edge_ref[pl.ds(EDGE + row, 1), :] = speed_ref[pl.ds(row * CELLS + a, 1), :]


def store_cells(
    where, low, high, up_is_first, low_ref, high_ref, first_block_ref, second_block_ref, next_ref, prev_ref
):
    low_ref[where, :] = low
    first_block_ref[where, :] = jnp.where(up_is_first, high, low)
    second_block_ref[where, :] = jnp.where(up_is_first, low, high)
    for out_ref in (high_ref, next_ref, prev_ref):
        out_ref[where, :] = high


def lines(count):
    return jax.ShapeDtypeStruct((count, AXIAL), jnp.float32)


def vmem(count):
    return [pl.BlockSpec(memory_space=pltpu.VMEM)] * count


def pack(field, speeds):
    row = lines(ROW_BYTES_ROWS)
    rim = lines(ROW_BYTES_ROWS + CELLS)
    edge = lines(EDGE + 8)
    return pl.pallas_call(
        pack_kernel,
        out_shape=(row, row, rim, rim, edge, edge),
        in_specs=vmem(2),
        out_specs=tuple(vmem(6)),
        compiler_params=pltpu.CompilerParams(vmem_limit_bytes=GRANT),
        name="pack",
    )(field, speeds)


def align_kernel(substep, shift_ref, weight_ref, own_ref, prev_ref, next_ref, _, direct_ref, cross_ref, row_ref):
    @pl.when(lax.axis_index("block") == lax.axis_size("block") - 1)
    def _():
        on_stator = lax.axis_index("region") == 1
        chosen = lax.broadcasted_iota(jnp.int32, (1, 2), 1) == substep
        residual = (jnp.sum(jnp.where(chosen, shift_ref[...], 0)) + CELLS) % STRIDE - CELLS
        weight, rest = [jnp.sum(jnp.where(chosen, weight_ref[pl.ds(row, 1), :], 0.0)) for row in range(2)]
        for place, part_ref in enumerate((prev_ref, own_ref, next_ref)):
            row_ref[pl.ds(place * ROW_BYTES_ROWS, ROW_BYTES_ROWS), :] = part_ref[pl.ds(0, ROW_BYTES_ROWS), :]
        first = CELLS + jnp.where(on_stator, residual, -residual - 1)
        later_weight = jnp.where(on_stator, rest, weight)

        def cell(index):
            return row_ref[pl.ds(pl.multiple_of((first + index) * SECTIONS, SECTIONS), SECTIONS), :]

        for a in range(CELLS):
            ghost = later_weight * cell(a + 1) + (1.0 - later_weight) * cell(a)
            direct_ref[pl.ds(a * OWN, OWN), :] = ghost[:OWN]
            cross_ref[pl.ds(a * CROSS, CROSS), :] = ghost[OWN:]


def align(substep, shifts, weights, own, from_prev, from_next, strain):
    return pl.pallas_call(
        functools.partial(align_kernel, substep),
        out_shape=(lines(CELLS * OWN), lines(CELLS * CROSS)),
        in_specs=vmem(6),
        out_specs=tuple(vmem(2)),
        scratch_shapes=[pltpu.VMEM((3 * ROW_BYTES_ROWS, AXIAL), jnp.float32)],
        compiler_params=pltpu.CompilerParams(vmem_limit_bytes=GRANT),
        name="align",
    )(shifts, weights, own, from_prev, from_next, strain)


def split_halves(value):
    high = value.astype(jnp.bfloat16)
    low = (value - high.astype(jnp.float32)).astype(jnp.bfloat16)
    return high, low


def substep_kernel(
    final,
    low_ref,
    high_ref,
    prev_ref,
    next_ref,
    first_block_ref,
    second_block_ref,
    direct_any,
    cross_any,
    prev_rim_ref,
    next_rim_ref,
    first_block_rim_ref,
    second_block_rim_ref,
    speed_ref,
    strain_ref,
    split_ref,
    merge_ref,
    *refs,
):
    if final:
        out_any, out_ref, *scratch = refs
    else:
        new_refs, scratch = refs[:6], refs[6:]
    coef_ref, top_ref, direct_ref, cross_ref, sems = scratch
    arrivals = [
        pltpu.make_async_copy(direct_any, direct_ref, sems.at[0]),
        pltpu.make_async_copy(cross_any, cross_ref, sems.at[1]),
    ]
    for copy in arrivals:
        copy.start()
    block = lax.axis_index("block")
    first_block = block == 0
    last_block = block == lax.axis_size("block") - 1
    up_is_first = is_even("block")

    def by_block(lines_of, first_ref=first_block_ref, second_ref=second_block_ref):
        one, two = first_ref[lines_of, :], second_ref[lines_of, :]
        return jnp.where(up_is_first, one, two), jnp.where(up_is_first, two, one)

    above_speed, below_speed = by_block(pl.ds(ROW_BYTES_ROWS, CELLS), first_block_rim_ref, second_block_rim_ref)

    for row in range(ROWS):
        azim = speed_ref[pl.ds(row * CELLS, CELLS), :]
        azim_next = jnp.concatenate([azim[1:], next_rim_ref[pl.ds(EDGE + row, 1), :]], axis=0)
        azim_prev = jnp.concatenate([prev_rim_ref[pl.ds(EDGE + row, 1), :], azim[:-1]], axis=0)
        azim_high = 0.5 * (azim + azim_next)
        azim_low = 0.5 * (azim_prev + azim)
        radial = speed_ref[pl.ds(STRIDE + row * CELLS, CELLS), :]
        if row == 0:
            other = speed_ref[pl.ds(STRIDE + CELLS, CELLS), :]
            radial_high = 0.5 * (radial + other)
            radial_low = jnp.where(first_block, 0.0, 0.5 * (below_speed + radial))
        else:
            other = speed_ref[pl.ds(STRIDE, CELLS), :]
            radial_high = jnp.where(last_block, radial, 0.5 * (radial + above_speed))
            radial_low = 0.5 * (other + radial)
        axial = speed_ref[pl.ds(2 * STRIDE + row * CELLS, CELLS), :]
        axial_high = 0.5 * (axial + pltpu.roll(axial, AXIAL - 1, 1))
        axial_low = pltpu.roll(axial_high, 1, 1)
        own = 0.0
        place = row * CELLS
        for number, (high, low) in enumerate(
            ((radial_high, radial_low), (azim_high, azim_low), (axial_high, axial_low))
        ):
            own = own + jnp.maximum(high, 0.0) - jnp.minimum(low, 0.0)
            coef_ref[2 * number, pl.ds(place, CELLS), :] = -TIME_STEP * jnp.minimum(high, 0.0)
            coef_ref[2 * number + 1, pl.ds(place, CELLS), :] = TIME_STEP * jnp.maximum(low, 0.0)
        coef_ref[6, pl.ds(place, CELLS), :] = 1.0 - TIME_STEP * own
        coef_ref[7, pl.ds(place, CELLS), :] = TIME_STEP * strain_ref[pl.ds(place, CELLS), :]

    split_high, split_low = split_halves(split_ref[...])
    merge_high, merge_low = split_halves(TIME_STEP * merge_ref[...])
    both_high = jnp.concatenate([split_high, merge_high], axis=0)
    both_low = jnp.concatenate([split_low, merge_low], axis=0)
    left = jnp.concatenate([both_high, both_high, both_low], axis=1)

    leaves = []
    for row in range(ROWS):
        own_ref = (low_ref, high_ref)[row]
        if row == ROWS - 1:
            for copy in arrivals:
                copy.wait()

            @pl.when(last_block)
            def _():
                for a in range(CELLS):
                    top_ref[pl.ds(a * SECTIONS, OWN), :] = direct_ref[pl.ds(a * OWN, OWN), :]
                    top_ref[pl.ds(a * SECTIONS + OWN, CROSS), :] = cross_ref[pl.ds(a * CROSS, CROSS), :]

            @pl.when(jnp.logical_not(last_block))
            def _():
                for a in range(CELLS):
                    top_ref[line(a), :] = by_block(line(a))[0]

        for pair in range(CELLS // 2):
            cells_of = [own_ref[line(2 * pair + i), :] for i in range(2)]
            wide = jnp.concatenate(cells_of, axis=1)
            high, low = split_halves(wide)
            right = jnp.concatenate([high, low, high], axis=0)
            products = jnp.dot(left, right, preferred_element_type=jnp.float32)
            for i in range(2):
                a = 2 * pair + i
                cells = cells_of[i]
                broken = products[:SECTIONS, i * AXIAL : (i + 1) * AXIAL]
                joined = products[SECTIONS:, i * AXIAL : (i + 1) * AXIAL]
                coef = lambda n: coef_ref[n, pl.ds(row * CELLS + a, 1), :]
                if row == 0:
                    outer, inner = high_ref[line(a), :], by_block(line(a))[1]
                else:
                    outer, inner = top_ref[line(a), :], low_ref[line(a), :]
                later = next_ref[line(0 if row else CELLS), :] if a == CELLS - 1 else own_ref[line(a + 1), :]
                earlier = prev_ref[line(CELLS - 1 if row else CELLS), :] if a == 0 else own_ref[line(a - 1), :]
                value = cells * (coef(6) + joined)
                value = value + coef(7) * broken
                value = value + (coef(0) * outer + coef(1) * inner)
                value = value + (coef(2) * later + coef(3) * earlier)
                value = value + (
                    coef(4) * pltpu.roll(cells, AXIAL - 1, 1) + coef(5) * pltpu.roll(cells, 1, 1)
                )
                if final:
                    out_lines = out_ref.reshape(SECTIONS * STRIDE, AXIAL)
                    out_lines[pl.ds(row * CELLS + a, SECTIONS, stride=STRIDE), :] = value
                elif row == 0:
                    new_refs[0][line(a), :] = value
                    if a in (0, CELLS - 1):
                        edge_ref = new_refs[4] if a else new_refs[5]
                        edge_ref[line(CELLS), :] = value
                else:
                    store_cells(line(a), new_refs[0][line(a), :], value, up_is_first, *new_refs)
        if final:
            rows = pl.ds(row * CELLS, CELLS)
            leave = pltpu.make_async_copy(out_ref.at[:, rows, :], out_any.at[:, rows, :], sems.at[2 + row])
            leave.start()
            leaves.append(leave)
    for leave in leaves:
        leave.wait()


def run_substep(final, *arrays):
    scratch = [
        pltpu.VMEM((8, STRIDE, AXIAL), jnp.float32),
        pltpu.VMEM((ROW_BYTES_ROWS, AXIAL), jnp.float32),
        pltpu.VMEM((CELLS * OWN, AXIAL), jnp.float32),
        pltpu.VMEM((CELLS * CROSS, AXIAL), jnp.float32),
        pltpu.SemaphoreType.DMA((2 + ROWS,)),
    ]
    if final:
        out_shape = jax.ShapeDtypeStruct((SECTIONS, STRIDE, AXIAL), jnp.float32)
        out_specs = pl.BlockSpec(memory_space=pltpu.HBM)
        scratch.insert(0, pltpu.VMEM(out_shape.shape, jnp.float32))
    else:
        out_shape = (lines(ROW_BYTES_ROWS),) * 4 + (lines(EDGE),) * 2
        out_specs = tuple(vmem(6))
    in_specs = vmem(len(arrays))
    in_specs[6:8] = [pl.BlockSpec(memory_space=pl.ANY)] * 2
    return pl.pallas_call(
        functools.partial(substep_kernel, final),
        out_shape=out_shape,
        in_specs=in_specs,
        out_specs=out_specs,
        scratch_shapes=scratch,
        compiler_params=pltpu.CompilerParams(vmem_limit_bytes=GRANT),
        name="substep",
    )(*arrays)


def turned(chips, direct, cross):
    count = lax.axis_size("sector") // 2

    def turn(steps, direct, cross):
        distance = min(steps, count - steps)
        if distance <= DIRECT_CHIPS or 2 * distance == count:
            cross = lax.ppermute(cross, AXES, turn_pairs(2 * steps, True))
            direct = lax.ppermute(direct, AXES, turn_pairs(2 * steps, True))
        else:
            cross = lax.ppermute(cross, AXES, turn_pairs(0, True))
            direct = lax.ppermute(direct, AXES, turn_pairs(2 * steps, True))
            cross = lax.ppermute(cross, AXES, turn_pairs(2 * steps, False))
        return direct, cross

    return lax.switch(chips, [functools.partial(turn, steps) for steps in range(count)], direct, cross)


def body(
    number_concentration,
    frame_motion_vector,
    strain_factor,
    splitting_kernel,
    merging_kernel,
    spinning_shift_history,
    nearest_coverage_fraction,
):
    field = number_concentration.reshape(SECTIONS * STRIDE, AXIAL)
    speeds = frame_motion_vector.reshape(3 * STRIDE, AXIAL)
    strain = strain_factor.reshape(STRIDE, AXIAL)
    shifts, weights = spinning_shift_history, nearest_coverage_fraction.reshape(1, 2)
    weights = jnp.concatenate([weights, 1.0 - weights], axis=0)
    arrays = pack(field, speeds)
    rims = None
    chips = lax.rem(lax.div(shifts + CELLS, STRIDE), lax.axis_size("sector") // 2)
    turns = lax.optimization_barrier((chips, lax.rev(chips, (0,))))
    for substep in range(2):
        low, high, first, second, to_next, to_prev = arrays
        from_prev = lax.ppermute(to_next, AXES, sector_pairs(1))
        from_next = lax.ppermute(to_prev, AXES, sector_pairs(-1))
        first = lax.ppermute(first, AXES, block_pairs(0))
        second = lax.ppermute(second, AXES, block_pairs(1))
        direct, cross = align(substep, shifts.reshape(1, 2), weights, high, from_prev, from_next, strain)
        direct, cross = turned(turns[substep][0], direct, cross)
        halos = (from_prev, from_next, first, second)
        rims = rims or halos
        arrays = run_substep(
            substep == 1,
            low,
            high,
            *halos,
            direct,
            cross,
            *rims,
            speeds,
            strain,
            splitting_kernel,
            merging_kernel,
        )
    return arrays.reshape(number_concentration.shape)


def solution(mesh):
    return jax.shard_map(
        body,
        mesh=mesh,
        in_specs=(
            P("region", None, "block", "sector", None),
            P("region", None, "block", "sector", None),
            P("region", "block", "sector", None),
            P(),
            P(),
            P(),
            P(),
        ),
        out_specs=P("region", None, "block", "sector", None),
        check_vma=False,
    )
```
